256 devices in a mesh: row: 16 (over y, x_hi, core), col: 16 (over z, x_lo).
Axes of the slice: x: 4 (x_hi: 2, x_lo: 2; x = x_hi * 2 + x_lo), y: 4, z: 8, core: 2. Of those that a mesh axis runs over, the one named last changes fastest.
Arguments:
- density: bfloat16 [8192, 8192], P('row', 'col'), may hold values from -1 to 1
- pattern: int32 [32, 32], P('row', 'col'), may hold values from 0 to 1, as said below
Outputs:
- purified: bfloat16 [8192, 8192], P('row', 'col')
The draws below stay inside these ranges and needn't reach their ends.
Inputs may be any that keep to these rules, and one draw needn't show every extreme that they name: pattern is symmetric with ones on its diagonal; no block row holds more than 12 ones, and some block row holds exactly 12.
All inputs are finite; a program needn't handle non-finite values.
Results may differ from the reference program's by a relative error of at most 0.0045.
Values may be sent and summed in bfloat16 or wider, within the bound.
A program may use at most 64 MiB of HBM per device.

```python
import jax
import jax.numpy as jnp
from jax import lax

NB = 32
N = 8192


def draw_pattern(key, part):
    key = jax.random.fold_in(key, 7)
    key_pick = jax.random.fold_in(key, 1)
    key_keep = jax.random.fold_in(key, 2)
    key_row = jax.random.fold_in(key, 3)
    count = NB // 8
    spread = NB // 2 - 2
    index = jnp.arange(spread, dtype=jnp.int32)
    score = jax.random.randint(key_pick, (spread,), 0, 2 * spread) - index
    order = jnp.argsort(-score)
    chosen = (order[:count] + 2).astype(jnp.int32)
    first = jnp.arange(NB, dtype=jnp.int32)[:, None]
    second = jnp.arange(NB, dtype=jnp.int32)[None, :]
    offset = (second - first) % NB
    inside = (offset == 0) | (offset == 1) | (offset == NB - 1) | (offset == NB // 2)
    matches = (offset[:, :, None] == chosen[None, None, :]) | (offset[:, :, None] == (NB - chosen)[None, None, :])
    inside = inside | jnp.any(matches, axis=2)
    raw = jax.random.randint(key_keep, (NB, NB), 0, 1000)
    both = raw + raw.T
    kept = both < 1400
    full_row = jax.random.randint(key_row, (), 0, NB)
    forced = (first == full_row) | (second == full_row) | (offset == 0)
    occupied = inside & (kept | forced)
    return occupied.astype(jnp.int32)


def steps_of(own_key, extent, shards, smallest, largest):
    loudness = 1.0
    for position, parts in shards:
        heights = jax.random.uniform(jax.random.fold_in(jax.random.fold_in(own_key, 6), position), (parts,), jnp.float32, smallest / len(shards), largest / len(shards))
        loudness = loudness * jnp.repeat(jnp.exp(heights), extent[position] // parts).reshape((-1,) + (1,) * (len(extent) - 1 - position))
    return loudness


def scatter_about(rng, shape, scale, bound, shards=(), kind=jnp.bfloat16):
    array = jax.random.normal(rng, shape, jnp.float32) * scale
    if len(shards) > 0:
        array = steps_of(rng, shape, shards, -0.22, 0.18) * array
    return jnp.clip(array, min=-bound, max=bound).astype(kind)


def setup_inputs(seed: int = 0) -> dict:
    streams_of = jax.random.split(jax.random.key(seed), 3)
    density = scatter_about(streams_of[0], (N, N), 0.0625, 1.0, ((0, 16), (1, 16)))
    pattern = draw_pattern(jax.random.fold_in(streams_of[2], 71), 0)
    return dict(density=density, pattern=pattern)


def block_filter(matrix, pattern):
    blocks = pattern.shape[0]
    size = matrix.shape[0] // blocks
    shaped = matrix.reshape(blocks, size, blocks, size)
    keep = pattern.astype(matrix.dtype)[:, None, :, None]
    return (shaped * keep).reshape(matrix.shape)


def reference(density, pattern):
    filtered = block_filter(density, pattern)
    wide = filtered.astype(jnp.float32)
    square = block_filter(jnp.dot(wide, wide, precision=lax.Precision.HIGHEST), pattern)
    square_low = square.astype(jnp.bfloat16).astype(jnp.float32)
    cube = block_filter(jnp.dot(square_low, wide, precision=lax.Precision.HIGHEST), pattern)
    return (3.0 * square - 2.0 * cube).astype(jnp.bfloat16)
```

```python
import functools

import jax
import jax.numpy as jnp
from jax import lax
from jax.experimental import pallas as pl
from jax.experimental.pallas import tpu as pltpu
from jax.sharding import PartitionSpec as P

MESH = pl.DeviceIdType.MESH
BF16 = jnp.bfloat16
F32 = jnp.float32
SIZE = 256
SLOTS = 12
NB = 32
GROUP = 16
PART = SIZE // GROUP


def place(x, y, z, core):
    return {"row": (y * 2 + lax.div(x, 2)) * 2 + core, "col": z * 2 + lax.rem(x, 2)}


def kernel(dens, patt, out, blocks, rr0, rr1, sr0, sr1, crecv, rp0, rp1, sp0, sp1, cp0, cp1, rhs0, rhs1, sf, sl, obuf, pmsg, prow, pcol, prow_s, pcol_s, nxt, idx, rank, a2a_send, row_recv, col_recv, pat_recv, pat_copy, s_send, s_recv, z_send, z_recv, mate_recv, c_send, c_recv, out_sem):
    rrecv, srecv, rpanel, spanel, cpanel, rhs = (rr0, rr1), (sr0, sr1), (rp0, rp1), (sp0, sp1), (cp0, cp1), (rhs0, rhs1)
    row, col = lax.axis_index("row"), lax.axis_index("col")
    y, xh, core = lax.div(row, 4), lax.rem(lax.div(row, 2), 2), lax.rem(row, 2)
    z, xl = lax.div(col, 2), lax.rem(col, 2)
    x = xh * 2 + xl
    pair = (y * 2 + xh) * 2
    part_z = z * 2 + core
    part_xy = y * 4 + x
    settled = xl == core

    def row_target(d):
        zz, cc = lax.rem(z + lax.div(d, 2), 8), lax.rem(core + d, 2)
        return zz * 2 + cc, {"row": pair + cc, "col": zz * 2 + core}

    def col_target(d):
        q = lax.rem(part_xy + d, GROUP)
        return q, {"row": lax.div(q, 2) * 2 + xl, "col": z * 2 + lax.rem(q, 2)}

    def mate_target(d):
        zz, cc = lax.rem(z + lax.div(d, 2), 8), lax.rem(core + d, 2)
        return zz * 2 + cc, {"row": pair + cc, "col": zz * 2 + xl}

    def z_side(s):
        return place(x, y, lax.rem(z + s + 8, 8), core)

    def xy_side(axis, s):
        if axis == 0:
            return place(lax.rem(x + s + 4, 4), y, z, core)
        return place(x, lax.rem(y + s + 4, 4), z, core)

    for i in range(2):
        for j in range(2):
            blocks[i, j] = dens[i, :, j * SIZE : (j + 1) * SIZE]

    barrier = pltpu.get_barrier_semaphore()

    def greet(d, _):
        @pl.when(jnp.logical_or(d != col, jnp.logical_not(settled)))
        def _():
            pl.semaphore_signal(barrier, 1, device_id={"row": part_xy, "col": d}, device_id_type=MESH)

        @pl.when(jnp.logical_or(d != row, jnp.logical_not(settled)))
        def _():
            pl.semaphore_signal(barrier, 1, device_id={"row": d, "col": part_z}, device_id_type=MESH)

        @pl.when(d != 0)
        def _():
            pl.semaphore_signal(barrier, 1, device_id=mate_target(d)[1], device_id_type=MESH)

        return 0

    lax.fori_loop(0, GROUP, greet, 0)
    for axis in range(2):
        for s in (1, -1):
            pl.semaphore_signal(barrier, 1, device_id=xy_side(axis, s), device_id_type=MESH)
    pl.semaphore_wait(barrier, jnp.where(settled, 30, 32) + 19)

    lane = lax.broadcasted_iota(jnp.int32, (1, 128), 1)
    entries = jnp.zeros((1, 128), jnp.int32)
    for i in range(2):
        for j in range(2):
            entries = jnp.where(lane == i * 2 + j, patt[i, j], entries)
    pmsg[...] = entries

    def send(src, dst, send_sem, recv_sem, device):
        pltpu.make_async_remote_copy(src_ref=src, dst_ref=dst, send_sem=send_sem, recv_sem=recv_sem, device_id=device, device_id_type=MESH).start()

    def deliver(d, src, dst, send_sem, recv_sem, device, always_self):
        here = d == 0 if always_self else jnp.logical_and(d == 0, settled)

        @pl.when(here)
        def _():
            pltpu.make_async_copy(src, dst, recv_sem).start()

        @pl.when(jnp.logical_not(here))
        def _():
            send(src, dst, send_sem, recv_sem, device)

    def wait_for(ref, sem):
        pltpu.make_async_copy(ref, ref, sem).wait()

    def send_patterns(d, _):
        _, device = row_target(d)
        deliver(d, pmsg, prow.at[col], a2a_send.at[2], pat_recv.at[0], device, False)
        _, device = col_target(d)
        deliver(d, pmsg, pcol.at[row], a2a_send.at[2], pat_recv.at[1], device, False)
        return 0

    lax.fori_loop(0, GROUP, send_patterns, 0)

    def send_rows(i):
        def body(n, _):
            d = lax.rem(n + 7, GROUP)
            s, device = row_target(d)
            deliver(d, blocks.at[i, :, pl.ds(pl.multiple_of(s * PART, PART), PART)], rrecv[i].at[pl.ds(2 * col, 2)], a2a_send.at[0], row_recv.at[i], device, False)
            return 0

        lax.fori_loop(0, GROUP, body, 0)

    def send_columns(n, _):
        d = lax.rem(n + 7, GROUP)
        q, device = col_target(d)
        deliver(d, dens.at[:, pl.ds(pl.multiple_of(q * PART, PART), PART)], crecv.at[pl.ds(2 * row, 2)], a2a_send.at[1], col_recv, device, False)
        return 0

    send_rows(0)
    lax.fori_loop(0, GROUP, send_columns, 0)
    send_rows(1)

    for received in (*rrecv, *srecv):
        received[NB] = jnp.zeros((PART, SIZE), BF16)
    crecv[NB] = jnp.zeros((PART, 2 * SIZE), BF16)
    for j in range(2):
        cpanel[j][:, SLOTS] = jnp.zeros((GROUP, PART, SIZE), BF16)

    wait_for(prow, pat_recv.at[0])
    wait_for(pcol, pat_recv.at[1])
    to_smem = [pltpu.make_async_copy(prow, prow_s, pat_copy.at[0]), pltpu.make_async_copy(pcol, pcol_s, pat_copy.at[1])]
    for c in to_smem:
        c.start()
    for c in to_smem:
        c.wait()

    def occupied(q, k):
        if q < 2:
            return prow_s[lax.div(k, 2), 0, q * 2 + lax.rem(k, 2)]
        return pcol_s[lax.div(k, 2), 0, lax.rem(k, 2) * 2 + (q - 2)]

    def backward(n, carry):
        k = NB - 1 - n
        later = []
        for q in range(4):
            nxt[q, k] = carry[q]
            later.append(carry[q] + occupied(q, k) * (k - carry[q]))
        return tuple(later)

    for q in range(4):
        nxt[q, NB] = NB
    first = lax.fori_loop(0, NB, backward, (jnp.int32(NB),) * 4)

    def forward(t, carry):
        later = []
        for q in range(4):
            idx[q, t] = carry[q]
            later.append(nxt[q, carry[q]])
        return tuple(later)

    lax.fori_loop(0, SLOTS, forward, first)

    def count(k, carry):
        later = []
        for j in range(2):
            is_on = occupied(2 + j, k)
            rank[j, k] = SLOTS + is_on * (carry[j] - SLOTS)
            later.append(carry[j] + is_on)
        return tuple(later)

    for j in range(2):
        rank[j, NB] = SLOTS
    lax.fori_loop(0, NB, count, (jnp.int32(0),) * 2)

    def unit(j, da, db):
        dx, dy = (da, db) if j == 0 else (db, da)
        return lax.rem(y + dy + 4, 4) * 4 + lax.rem(x + dx + 4, 4)

    order = {0: 0, -1: 1, 1: 2, 2: 3}

    def column_send(j, q, half, axis, s, n):
        slots = pl.ds(0, SLOTS) if half is None else pl.ds(half * (SLOTS // 2), SLOTS // 2)
        ref = cpanel[j].at[q, slots]
        send(ref, ref, c_send.at[j], c_recv.at[j, n], xy_side(axis, s))

    def column_wait(j, q, half, n):
        slots = pl.ds(0, SLOTS) if half is None else pl.ds(half * (SLOTS // 2), SLOTS // 2)
        wait_for(cpanel[j].at[q, slots], c_recv.at[j, n])

    def column_along(j, da):
        for way, s in enumerate((1, -1)):
            column_send(j, unit(j, da, 0), None, 1 - j, s, 4 + order[da] * 2 + way)

    def column_own(j):
        def body(t, _):
            cpanel[j][part_xy, t] = crecv[idx[2 + j, t], :, j * SIZE : (j + 1) * SIZE]
            return 0

        lax.fori_loop(0, SLOTS, body, 0)

    def column_first(j):
        for way, s in enumerate((1, -1)):
            column_send(j, unit(j, 0, 0), None, j, s, way)

    def column_near(j):
        for way, s in enumerate((1, -1)):
            column_wait(j, unit(j, -s, 0), None, way)
            column_send(j, unit(j, -s, 0), way, j, s, 2 + way)
        column_along(j, -1)
        column_along(j, 1)

    def column_far(j):
        for way in range(2):
            column_wait(j, unit(j, 2, 0), way, 2 + way)
        column_along(j, 2)

    def column_second(j, da):
        for way, s in enumerate((1, -1)):
            column_wait(j, unit(j, da, -s), None, 4 + order[da] * 2 + way)
            if (da in (0, -1)) == (s == 1):
                column_send(j, unit(j, da, -s), None, 1 - j, s, 12 + order[da])

    def column_last(j):
        for da in order:
            column_wait(j, unit(j, da, 2), None, 12 + order[da])

    def ring(i, stage):
        panel = (rpanel, spanel)[stage][i]
        sem = z_recv.at[stage, i]

        def ref(d, half=None):
            here = lax.rem(z + d + 8, 8) * 2 + core
            return panel.at[here] if half is None else panel.at[here, :, pl.ds(half * (SLOTS // 2 * SIZE), SLOTS // 2 * SIZE)]

        def to_mate(d):
            send(ref(d), ref(d), z_send.at[stage, i], mate_recv.at[stage, i], {"row": pair + 1 - core, "col": col})

        def compact(received):
            def body(t, _):
                panel[part_z, :, pl.ds(pl.multiple_of(t * SIZE, SIZE), SIZE)] = received[idx[i, t]]
                return 0

            lax.fori_loop(0, SLOTS, body, 0)

        def start():
            for way, s in enumerate((1, -1)):
                send(ref(0), ref(0), z_send.at[stage, i], sem.at[way, 0], z_side(s))
            to_mate(0)

        def hop(d):
            for way, s in enumerate((1, -1)):
                wait_for(ref(-s * d), sem.at[way, d - 1])
                half = None if d < 3 else way
                send(ref(-s * d, half), ref(-s * d, half), z_send.at[stage, i], sem.at[way, d], z_side(s))
            for s in (1, -1):
                to_mate(-s * d)

        def last():
            for way in range(2):
                wait_for(ref(4, way), sem.at[way, 3])
            to_mate(4)

        def finish():
            wait_for(panel.at[pl.ds(0, 8)], mate_recv.at[stage, i])

        return compact, start, hop, last, finish

    rows = [ring(0, 0), ring(1, 0)]

    def row_own(i):
        compact, start, _, _, _ = rows[i]
        wait_for(rrecv[i].at[pl.ds(0, NB)], row_recv.at[i])
        compact(rrecv[i])
        start()

    wait_for(crecv.at[pl.ds(0, NB)], col_recv)
    column_own(0)
    column_first(0)
    column_own(1)
    column_first(1)
    column_along(0, 0)
    column_along(1, 0)
    row_own(0)
    column_near(0)
    column_near(1)
    row_own(1)
    column_second(0, 0)
    column_second(1, 0)
    column_far(0)
    column_far(1)
    rows[0][2](1)
    column_second(0, -1)
    column_second(1, -1)
    rows[1][2](1)
    rows[0][2](2)
    column_second(0, 1)
    column_second(1, 1)
    rows[1][2](2)
    rows[0][2](3)
    column_second(0, 2)
    column_second(1, 2)
    rows[1][2](3)
    rows[0][3]()
    column_last(0)
    column_last(1)

    def gather_rhs(i):
        def body(t, _):
            k = idx[i, t]
            for j in range(2):
                block = cpanel[j][:, rank[j, k]]
                rhs[i][pl.ds(pl.multiple_of(t * SIZE, SIZE), SIZE), j * SIZE : (j + 1) * SIZE] = block.reshape(SIZE, SIZE)
            return 0

        lax.fori_loop(0, SLOTS, body, 0)

    def product(panel, i):
        whole = jnp.dot(panel[i][...].reshape(SIZE, SLOTS * SIZE), rhs[i][...], preferred_element_type=F32)
        keep = [prow_s[part_z, 0, i * 2 + j].astype(F32) for j in range(2)]
        return jnp.concatenate([whole[:, :SIZE] * keep[0], whole[:, SIZE:] * keep[1]], axis=1)

    def square(i):
        value = product(rpanel, i)
        sf[i] = value
        for j in range(2):
            sl[i, j] = value[:, j * SIZE : (j + 1) * SIZE].astype(BF16)

        def body(n, _):
            d = lax.rem(n + 7, GROUP)
            s, device = mate_target(d)
            deliver(d, sl.at[i, :, pl.ds(pl.multiple_of(s * PART, PART), PART)], srecv[i].at[pl.ds(2 * part_z, 2)], s_send.at[i], s_recv.at[i], device, True)
            return 0

        lax.fori_loop(0, GROUP, body, 0)

    gather_rhs(0)
    rows[0][4]()
    square(0)
    rows[1][3]()
    gather_rhs(1)
    rows[1][4]()
    square(1)

    squares = [ring(0, 1), ring(1, 1)]
    for i in range(2):
        wait_for(srecv[i].at[pl.ds(0, NB)], s_recv.at[i])
        squares[i][0](srecv[i])
        squares[i][1]()
    for d in (1, 2, 3):
        for i in range(2):
            squares[i][2](d)

    def cube(i):
        squares[i][3]()
        squares[i][4]()
        value = (3.0 * sf[i] - 2.0 * product(spanel, i)).astype(BF16)

        @pl.when(settled)
        def _():
            out[i] = value

        @pl.when(jnp.logical_not(settled))
        def _():
            obuf[i] = value
            send(obuf.at[i], out.at[i], out_sem.at[0, i], out_sem.at[1, i], {"row": pair + xl, "col": part_z})

    cube(0)
    cube(1)

    @pl.when(jnp.logical_not(settled))
    def _():
        for i in range(2):
            wait_for(out.at[i], out_sem.at[1, i])
            wait_for(obuf.at[i], out_sem.at[0, i])
        for i in range(2):
            wait_for(rrecv[i].at[pl.ds(0, 2)], a2a_send.at[0])
        wait_for(crecv.at[pl.ds(0, 2)], a2a_send.at[1])
        wait_for(prow.at[0], a2a_send.at[2])
        wait_for(pcol.at[0], a2a_send.at[2])

    for i in range(2):
        wait_for(rrecv[i].at[pl.ds(0, 30)], a2a_send.at[0])
    wait_for(crecv.at[pl.ds(0, 30)], a2a_send.at[1])
    wait_for(prow.at[pl.ds(1, 15)], a2a_send.at[2])
    wait_for(pcol.at[pl.ds(1, 15)], a2a_send.at[2])
    for i in range(2):
        wait_for(srecv[i].at[pl.ds(0, 30)], s_send.at[i])
        for stage in range(2):
            wait_for((rpanel, spanel)[stage][i].at[pl.ds(0, 15)], z_send.at[stage, i])
        wait_for(cpanel[i].at[pl.ds(0, 15), pl.ds(0, SLOTS)], c_send.at[i])


def shards(density, pattern):
    wide = SLOTS * SIZE
    vmem, smem, dma = pltpu.VMEM, pltpu.SMEM, pltpu.SemaphoreType.DMA
    received = vmem((NB + 1, PART, SIZE), BF16)
    panel = vmem((GROUP, PART, wide), BF16)
    purified = pl.pallas_call(
        kernel,
        out_shape=jax.ShapeDtypeStruct((2, SIZE, 2 * SIZE), BF16),
        in_specs=[pl.BlockSpec(memory_space=vmem), pl.BlockSpec(memory_space=smem)],
        out_specs=pl.BlockSpec(memory_space=vmem),
        scratch_shapes=[
            vmem((2, 2, SIZE, SIZE), BF16),
            received, received, received, received,
            vmem((NB + 1, PART, 2 * SIZE), BF16),
            panel, panel, panel, panel,
            vmem((GROUP, SLOTS + 1, PART, SIZE), BF16),
            vmem((GROUP, SLOTS + 1, PART, SIZE), BF16),
            vmem((wide, 2 * SIZE), BF16),
            vmem((wide, 2 * SIZE), BF16),
            vmem((2, SIZE, 2 * SIZE), F32),
            vmem((2, 2, SIZE, SIZE), BF16),
            vmem((2, SIZE, 2 * SIZE), BF16),
            vmem((1, 128), jnp.int32),
            vmem((GROUP, 1, 128), jnp.int32),
            vmem((GROUP, 1, 128), jnp.int32),
            smem((GROUP, 1, 128), jnp.int32),
            smem((GROUP, 1, 128), jnp.int32),
            smem((4, NB + 1), jnp.int32),
            smem((4, SLOTS), jnp.int32),
            smem((2, NB + 1), jnp.int32),
            dma((3,)), dma((2,)), dma, dma((2,)), dma((2,)),
            dma((2,)), dma((2,)), dma((2, 2)), dma((2, 2, 2, 4)), dma((2, 2)),
            dma((2,)), dma((2, 16)), dma((2, 2)),
        ],
        compiler_params=pltpu.CompilerParams(collective_id=0, has_side_effects=True, vmem_limit_bytes=48 * 2**20),
        name="purify",
    )(density.reshape(2, SIZE, 2 * SIZE), pattern)
    return purified.reshape(2 * SIZE, 2 * SIZE)


def solution(mesh):
    return jax.shard_map(
        shards,
        mesh=mesh,
        in_specs=(P("row", "col"), P("row", "col")),
        out_specs=P("row", "col"),
        check_vma=False,
    )
```

```python
import functools

import jax
import jax.numpy as jnp
from jax import lax
from jax.experimental import pallas as pl
from jax.experimental.pallas import tpu as pltpu
from jax.sharding import PartitionSpec as P

MESH = pl.DeviceIdType.MESH
BF16 = jnp.bfloat16
F32 = jnp.float32
SIZE = 256
SLOTS = 12
HALF = SIZE // 2
NB = 32
GROUP = 16
PART = SIZE // GROUP


def place(x, y, z, core):
    return {"row": (y * 2 + lax.div(x, 2)) * 2 + core, "col": z * 2 + lax.rem(x, 2)}


def kernel(dens, patt_hbm, out, blocks, patt, rr0, rr1, rr2, rr3, sr0, sr1, sr2, sr3, crecv, panel, cp0, cp1, rhs, sf, cf, sl, obuf, pmsg, prow, pcol, prow_s, pcol_s, nxt, idx, rank, load_sem, a2a_send, row_recv, col_recv, pat_recv, pat_copy, s_send, s_recv, z_send, z_recv, mate_recv, c_send, c_recv, out_sem):
    rrecv, srecv, cpanel = (rr0, rr1, rr2, rr3), (sr0, sr1, sr2, sr3), (cp0, cp1)
    row, col = lax.axis_index("row"), lax.axis_index("col")
    y, xh, core = lax.div(row, 4), lax.rem(lax.div(row, 2), 2), lax.rem(row, 2)
    z, xl = lax.div(col, 2), lax.rem(col, 2)
    x = xh * 2 + xl
    pair = (y * 2 + xh) * 2
    part_z = z * 2 + core
    part_xy = y * 4 + x
    settled = xl == core

    def row_target(d):
        zz, cc = lax.rem(z + lax.div(d, 2), 8), lax.rem(core + d, 2)
        return zz * 2 + cc, {"row": pair + cc, "col": zz * 2 + core}

    def col_target(d):
        q = lax.rem(part_xy + d, GROUP)
        return q, {"row": lax.div(q, 2) * 2 + xl, "col": z * 2 + lax.rem(q, 2)}

    def mate_target(d):
        zz, cc = lax.rem(z + lax.div(d, 2), 8), lax.rem(core + d, 2)
        return zz * 2 + cc, {"row": pair + cc, "col": zz * 2 + xl}

    def z_side(s):
        return place(x, y, lax.rem(z + s + 8, 8), core)

    def xy_side(axis, s):
        if axis == 0:
            return place(lax.rem(x + s + 4, 4), y, z, core)
        return place(x, lax.rem(y + s + 4, 4), z, core)

    loads = [pltpu.make_async_copy(patt_hbm, patt, load_sem.at[0])]
    for i in range(2):
        for j in range(2):
            loads.append(pltpu.make_async_copy(dens.at[i, :, pl.ds(j * SIZE, SIZE)], blocks.at[i, j], load_sem.at[1 + 2 * i + j]))
    for load in loads:
        load.start()

    barrier = pltpu.get_barrier_semaphore()

    def greet(device):
        pl.semaphore_signal(barrier, 1, device_id=device, device_id_type=MESH)

    for d in range(GROUP):
        @pl.when(jnp.logical_or(d != col, jnp.logical_not(settled)))
        def _():
            greet({"row": part_xy, "col": d})

    for d in range(GROUP):
        @pl.when(jnp.logical_or(d != row, jnp.logical_not(settled)))
        def _():
            greet({"row": d, "col": part_z})

    for d in range(1, GROUP):
        greet(mate_target(d)[1])
    for axis in range(2):
        for s in (1, -1):
            greet(xy_side(axis, s))
    for load in loads:
        load.wait()
    pl.semaphore_wait(barrier, jnp.where(settled, 30, 32) + 19)

    lane = lax.broadcasted_iota(jnp.int32, (1, 128), 1)
    entries = jnp.zeros((1, 128), jnp.int32)
    for i in range(2):
        for j in range(2):
            entries = jnp.where(lane == i * 2 + j, patt[i, j], entries)
    pmsg[...] = entries

    def send(src, dst, send_sem, recv_sem, device):
        pltpu.make_async_remote_copy(src_ref=src, dst_ref=dst, send_sem=send_sem, recv_sem=recv_sem, device_id=device, device_id_type=MESH).start()

    def deliver(d, src, dst, send_sem, recv_sem, device, always_self):
        here = d == 0 if always_self else jnp.logical_and(d == 0, settled)

        @pl.when(here)
        def _():
            pltpu.make_async_copy(src, dst, recv_sem).start()

        @pl.when(jnp.logical_not(here))
        def _():
            send(src, dst, send_sem, recv_sem, device)

    def wait_for(ref, sem):
        pltpu.make_async_copy(ref, ref, sem).wait()

    def send_patterns(d, _):
        _, device = row_target(d)
        deliver(d, pmsg, prow.at[col], a2a_send.at[2], pat_recv.at[0], device, False)
        _, device = col_target(d)
        deliver(d, pmsg, pcol.at[row], a2a_send.at[2], pat_recv.at[1], device, False)
        return 0

    lax.fori_loop(0, GROUP, send_patterns, 0)

    def half(h):
        return pl.ds(h * HALF, HALF)

    def send_rows(c):
        def body(n, _):
            d = lax.rem(n + 7, GROUP)
            s, device = row_target(d)
            deliver(d, blocks.at[c // 2, :, pl.ds(pl.multiple_of(s * PART, PART), PART), half(c % 2)], rrecv[c].at[pl.ds(2 * col, 2)], a2a_send.at[0], row_recv.at[c], device, False)
            return 0

        lax.fori_loop(0, GROUP, body, 0)

    def send_columns(n, _):
        d = lax.rem(n + 7, GROUP)
        q, device = col_target(d)
        deliver(d, dens.at[:, pl.ds(pl.multiple_of(q * PART, PART), PART)], crecv.at[pl.ds(2 * row, 2)], a2a_send.at[1], col_recv, device, False)
        return 0

    send_rows(0)
    lax.fori_loop(0, GROUP, send_columns, 0)
    for c in range(1, 4):
        send_rows(c)

    for received in (*rrecv, *srecv):
        received[NB] = jnp.zeros((PART, HALF), BF16)
    crecv[NB] = jnp.zeros((PART, 2 * SIZE), BF16)
    for j in range(2):
        cpanel[j][:, SLOTS] = jnp.zeros((GROUP, PART, SIZE), BF16)

    wait_for(prow, pat_recv.at[0])
    wait_for(pcol, pat_recv.at[1])
    to_smem = [pltpu.make_async_copy(prow, prow_s, pat_copy.at[0]), pltpu.make_async_copy(pcol, pcol_s, pat_copy.at[1])]
    for c in to_smem:
        c.start()
    for c in to_smem:
        c.wait()

    def occupied(q, k):
        if q < 2:
            return prow_s[lax.div(k, 2), 0, q * 2 + lax.rem(k, 2)]
        return pcol_s[lax.div(k, 2), 0, lax.rem(k, 2) * 2 + (q - 2)]

    def backward(n, carry):
        k = NB - 1 - n
        later = []
        for q in range(4):
            nxt[q, k] = carry[q]
            later.append(carry[q] + occupied(q, k) * (k - carry[q]))
        return tuple(later)

    for q in range(4):
        nxt[q, NB] = NB
    first = lax.fori_loop(0, NB, backward, (jnp.int32(NB),) * 4)

    def forward(t, carry):
        later = []
        for q in range(4):
            idx[q, t] = carry[q]
            later.append(nxt[q, carry[q]])
        return tuple(later)

    lax.fori_loop(0, SLOTS, forward, first)

    def count(k, carry):
        later = []
        for j in range(2):
            is_on = occupied(2 + j, k)
            rank[j, k] = SLOTS + is_on * (carry[j] - SLOTS)
            later.append(carry[j] + is_on)
        return tuple(later)

    for j in range(2):
        rank[j, NB] = SLOTS
    lax.fori_loop(0, NB, count, (jnp.int32(0),) * 2)

    def unit(j, da, db):
        dx, dy = (da, db) if j == 0 else (db, da)
        return lax.rem(y + dy + 4, 4) * 4 + lax.rem(x + dx + 4, 4)

    order = {0: 0, -1: 1, 1: 2, 2: 3}

    def column_send(j, q, half, axis, s, n):
        slots = pl.ds(0, SLOTS) if half is None else pl.ds(half * (SLOTS // 2), SLOTS // 2)
        ref = cpanel[j].at[q, slots]
        send(ref, ref, c_send.at[j], c_recv.at[j, n], xy_side(axis, s))

    def column_wait(j, q, half, n):
        slots = pl.ds(0, SLOTS) if half is None else pl.ds(half * (SLOTS // 2), SLOTS // 2)
        wait_for(cpanel[j].at[q, slots], c_recv.at[j, n])

    def column_along(j, da):
        for way, s in enumerate((1, -1)):
            column_send(j, unit(j, da, 0), None, 1 - j, s, 4 + order[da] * 2 + way)

    def column_own(j):
        def body(t, _):
            cpanel[j][part_xy, t] = crecv[idx[2 + j, t], :, j * SIZE : (j + 1) * SIZE]
            return 0

        lax.fori_loop(0, SLOTS, body, 0)

    def column_start():
        wait_for(crecv.at[pl.ds(0, NB)], col_recv)
        for j in range(2):
            column_own(j)
            for way, s in enumerate((1, -1)):
                column_send(j, unit(j, 0, 0), None, j, s, way)
        for j in range(2):
            column_along(j, 0)

    def column_near(j, s):
        way = (1 - s) // 2
        column_wait(j, unit(j, -s, 0), None, way)
        column_send(j, unit(j, -s, 0), way, j, s, 2 + way)
        column_along(j, -s)

    def column_far(j):
        for way in range(2):
            column_wait(j, unit(j, 2, 0), way, 2 + way)
        column_along(j, 2)

    def column_second(j, da, s):
        column_wait(j, unit(j, da, -s), None, 4 + order[da] * 2 + (1 - s) // 2)
        if (da in (0, -1)) == (s == 1):
            column_send(j, unit(j, da, -s), None, 1 - j, s, 12 + order[da])

    def column_last(j):
        for da in order:
            column_wait(j, unit(j, da, 2), None, 12 + order[da])

    def slices(stage, c, d, part=None):
        here = panel.at[stage, c, lax.rem(z + d + 8, 8) * 2 + core]
        return here if part is None else here.at[:, pl.ds(part * (SLOTS // 2 * HALF), SLOTS // 2 * HALF)]

    def ring_send(stage, c, d, s, part=None):
        ref = slices(stage, c, -s * d, part)
        send(ref, ref, z_send.at[stage, c], z_recv.at[stage, c, (1 - s) // 2, d], z_side(s))

    def to_mate(stage, c, d):
        ref = slices(stage, c, d)
        send(ref, ref, z_send.at[stage, c], mate_recv.at[stage, c], {"row": pair + 1 - core, "col": col})

    def ring_start(stage, c):
        received = (rrecv, srecv)[stage][c]
        wait_for(received.at[pl.ds(0, NB)], (row_recv, s_recv)[stage].at[c])

        def body(t, _):
            panel[stage, c, part_z, :, pl.ds(pl.multiple_of(t * HALF, HALF), HALF)] = received[idx[c // 2, t]]
            return 0

        lax.fori_loop(0, SLOTS, body, 0)
        for s in (1, -1):
            ring_send(stage, c, 0, s)
        to_mate(stage, c, 0)

    def ring_hop(stage, c, d):
        for way, s in enumerate((1, -1)):
            wait_for(slices(stage, c, -s * d), z_recv.at[stage, c, way, d - 1])
            ring_send(stage, c, d, s, None if d < 3 else way)
        for s in (1, -1):
            to_mate(stage, c, -s * d)

    def ring_last(stage, c):
        for way in range(2):
            wait_for(slices(stage, c, 4, way), z_recv.at[stage, c, way, 3])
        to_mate(stage, c, 4)

    def ring_end(stage, c):
        wait_for(panel.at[stage, c, pl.ds(0, 8)], mate_recv.at[stage, c])

    def gather_rhs(i):
        def body(t, _):
            k = idx[i, t]
            for j in range(2):
                slot = rank[j, k]
                for h in range(2):
                    block = cpanel[j][h * 8 : h * 8 + 8, slot]
                    rhs[2 * i + h, pl.ds(pl.multiple_of(t * HALF, HALF), HALF), j * SIZE : (j + 1) * SIZE] = block.reshape(HALF, SIZE)
            return 0

        lax.fori_loop(0, SLOTS, body, 0)

    def product(stage, c):
        ring_end(stage, c)
        return jnp.dot(panel[stage, c].reshape(SIZE, SLOTS * HALF), rhs[c], preferred_element_type=F32)

    def keep(i, j):
        return prow_s[part_z, 0, i * 2 + j].astype(F32)

    def square(c):
        i = c // 2
        if c % 2 == 0:
            sf[i] = product(0, c)
            return
        value = sf[i] + product(0, c)
        for j in range(2):
            kept = value[:, j * SIZE : (j + 1) * SIZE] * keep(i, j)
            sf[i, :, j * SIZE : (j + 1) * SIZE] = kept
            sl[i, j] = kept.astype(BF16)
        for h in range(2):
            def body(n, _):
                d = lax.rem(n + 7, GROUP)
                s, device = mate_target(d)
                deliver(d, sl.at[i, :, pl.ds(pl.multiple_of(s * PART, PART), PART), half(h)], srecv[2 * i + h].at[pl.ds(2 * part_z, 2)], s_send.at[i], s_recv.at[2 * i + h], device, True)
                return 0

            lax.fori_loop(0, GROUP, body, 0)

    def cube(c):
        i = c // 2
        if c % 2 == 0:
            cf[i] = product(1, c)
            return
        whole = cf[i] + product(1, c)
        value = jnp.concatenate([whole[:, j * SIZE : (j + 1) * SIZE] * keep(i, j) for j in range(2)], axis=1)
        value = (3.0 * sf[i] - 2.0 * value).astype(BF16)

        @pl.when(settled)
        def _():
            out[i] = value

        @pl.when(jnp.logical_not(settled))
        def _():
            obuf[i] = value
            send(obuf.at[i], out.at[i], out_sem.at[0, i], out_sem.at[1, i], {"row": pair + xl, "col": part_z})

    ring_start(0, 0)
    column_start()
    ring_start(0, 1)
    ring_start(0, 2)
    column_near(0, 1)
    column_near(0, -1)
    ring_hop(0, 0, 1)
    column_near(1, 1)
    column_near(1, -1)
    ring_hop(0, 1, 1)
    ring_start(0, 3)
    ring_hop(0, 2, 1)
    column_second(1, 0, 1)
    ring_hop(0, 0, 2)
    column_second(1, 0, -1)
    column_second(0, 0, 1)
    column_second(0, 0, -1)
    ring_hop(0, 1, 2)
    column_far(0)
    column_second(0, -1, 1)
    ring_hop(0, 3, 1)
    column_second(0, -1, -1)
    column_second(1, -1, 1)
    column_second(1, -1, -1)
    column_second(0, 1, 1)
    ring_hop(0, 2, 2)
    column_second(0, 1, -1)
    column_second(1, 1, 1)
    column_second(1, 1, -1)
    ring_hop(0, 0, 3)
    column_far(1)
    ring_hop(0, 1, 3)
    column_second(0, 2, -1)
    ring_hop(0, 3, 2)
    ring_hop(0, 2, 3)
    ring_last(0, 0)
    column_second(0, 2, 1)
    ring_last(0, 1)
    ring_hop(0, 3, 3)
    ring_last(0, 2)
    column_second(1, 2, 1)
    column_second(1, 2, -1)
    column_last(0)
    ring_last(0, 3)
    column_last(1)
    gather_rhs(0)
    square(0)
    square(1)
    gather_rhs(1)
    square(2)
    square(3)
    ring_start(1, 0)
    ring_start(1, 1)
    ring_start(1, 2)
    ring_hop(1, 0, 1)
    ring_hop(1, 1, 1)
    ring_start(1, 3)
    ring_hop(1, 2, 1)
    ring_hop(1, 0, 2)
    ring_hop(1, 1, 2)
    ring_hop(1, 3, 1)
    ring_hop(1, 2, 2)
    ring_hop(1, 0, 3)
    ring_hop(1, 1, 3)
    ring_hop(1, 3, 2)
    ring_hop(1, 2, 3)
    ring_last(1, 0)
    ring_last(1, 1)
    ring_hop(1, 3, 3)
    ring_last(1, 2)
    cube(0)
    cube(1)
    ring_last(1, 3)
    cube(2)
    cube(3)

    @pl.when(jnp.logical_not(settled))
    def _():
        for i in range(2):
            wait_for(out.at[i], out_sem.at[1, i])
            wait_for(obuf.at[i], out_sem.at[0, i])
        for c in range(4):
            wait_for(rrecv[c].at[pl.ds(0, 2)], a2a_send.at[0])
        wait_for(crecv.at[pl.ds(0, 2)], a2a_send.at[1])
        wait_for(prow.at[0], a2a_send.at[2])
        wait_for(pcol.at[0], a2a_send.at[2])

    for c in range(4):
        wait_for(rrecv[c].at[pl.ds(0, 30)], a2a_send.at[0])
    wait_for(crecv.at[pl.ds(0, 30)], a2a_send.at[1])
    wait_for(prow.at[pl.ds(1, 15)], a2a_send.at[2])
    wait_for(pcol.at[pl.ds(1, 15)], a2a_send.at[2])
    for c in range(4):
        wait_for(srecv[c].at[pl.ds(0, 30)], s_send.at[c // 2])
        for stage in range(2):
            wait_for(panel.at[stage, c, pl.ds(0, 15)], z_send.at[stage, c])
    for j in range(2):
        wait_for(cpanel[j].at[pl.ds(0, 15), pl.ds(0, SLOTS)], c_send.at[j])


def shards(density, pattern):
    vmem, smem, dma = pltpu.VMEM, pltpu.SMEM, pltpu.SemaphoreType.DMA
    received = [vmem((NB + 1, PART, HALF), BF16)] * 4
    panel = vmem((GROUP, SLOTS + 1, PART, SIZE), BF16)
    purified = pl.pallas_call(
        kernel,
        out_shape=jax.ShapeDtypeStruct((2, SIZE, 2 * SIZE), BF16),
        in_specs=[pl.BlockSpec(memory_space=pl.ANY)] * 2,
        out_specs=pl.BlockSpec(memory_space=vmem),
        scratch_shapes=[
            vmem((2, 2, SIZE, SIZE), BF16),
            smem((2, 2), jnp.int32),
            *received, *received,
            vmem((NB + 1, PART, 2 * SIZE), BF16),
            vmem((2, 4, GROUP, PART, SLOTS * HALF), BF16),
            panel, panel,
            vmem((4, SLOTS * HALF, 2 * SIZE), BF16),
            vmem((2, SIZE, 2 * SIZE), F32),
            vmem((2, SIZE, 2 * SIZE), F32),
            vmem((2, 2, SIZE, SIZE), BF16),
            vmem((2, SIZE, 2 * SIZE), BF16),
            vmem((1, 128), jnp.int32),
            vmem((GROUP, 1, 128), jnp.int32),
            vmem((GROUP, 1, 128), jnp.int32),
            smem((GROUP, 1, 128), jnp.int32),
            smem((GROUP, 1, 128), jnp.int32),
            smem((4, NB + 1), jnp.int32),
            smem((4, SLOTS), jnp.int32),
            smem((2, NB + 1), jnp.int32),
            dma((5,)), dma((3,)), dma((4,)), dma, dma((2,)), dma((2,)),
            dma((2,)), dma((4,)), dma((2, 4)), dma((2, 4, 2, 4)), dma((2, 4)),
            dma((2,)), dma((2, 16)), dma((2, 2)),
        ],
        compiler_params=pltpu.CompilerParams(collective_id=0, has_side_effects=True, vmem_limit_bytes=48 * 2**20),
        name="purify",
    )(density.reshape(2, SIZE, 2 * SIZE), pattern)
    return purified.reshape(2 * SIZE, 2 * SIZE)


def solution(mesh):
    return jax.shard_map(
        shards,
        mesh=mesh,
        in_specs=(P("row", "col"), P("row", "col")),
        out_specs=P("row", "col"),
        check_vma=False,
    )
```

```python
import functools

import jax
import jax.numpy as jnp
from jax import lax
from jax.experimental import pallas as pl
from jax.experimental.pallas import tpu as pltpu
from jax.sharding import PartitionSpec as P

MESH = pl.DeviceIdType.MESH
BF16 = jnp.bfloat16
F32 = jnp.float32
SIZE = 256
SLOTS = 12
HALF = SIZE // 2
NB = 32
GROUP = 16
PART = SIZE // GROUP


def place(x, y, z, core):
    return {"row": (y * 2 + lax.div(x, 2)) * 2 + core, "col": z * 2 + lax.rem(x, 2)}


def kernel(dens, patt_hbm, out, blocks, patt, rr0, rr1, rr2, rr3, sr0, sr1, sr2, sr3, crecv, panel, square_panel, cp0, cp1, cp2, cp3, rhs, sf, smate, cf, sl, obuf, pmsg, prow, pcol, pmate, prow_s, pcol_s, pmate_s, nxt, idx, rank, load_sem, a2a_send, row_recv, col_recv, pat_recv, pat_copy, s_send, s_recv, z_send, z_recv, mate_recv, share_send, share_recv, c_send, c_recv, out_send, out_recv):
    rrecv, srecv, cpanel = (rr0, rr1, rr2, rr3), (sr0, sr1, sr2, sr3), (cp0, cp1, cp2, cp3)
    row, col = lax.axis_index("row"), lax.axis_index("col")
    y, xh, core = lax.div(row, 4), lax.rem(lax.div(row, 2), 2), lax.rem(row, 2)
    z, xl = lax.div(col, 2), lax.rem(col, 2)
    x = xh * 2 + xl
    pair = (y * 2 + xh) * 2
    part_z = z * 2 + core
    part_xy = y * 4 + x
    settled = xl == core

    def row_target(d):
        zz, cc = lax.rem(z + lax.div(d, 2), 8), lax.rem(core + d, 2)
        return zz * 2 + cc, {"row": pair + cc, "col": zz * 2 + core}

    def col_target(d):
        q = lax.rem(part_xy + d, GROUP)
        return q, {"row": lax.div(q, 2) * 2 + xl, "col": z * 2 + lax.rem(q, 2)}

    def mate_target(d):
        zz, cc = lax.rem(z + lax.div(d, 2), 8), lax.rem(core + d, 2)
        return zz * 2 + cc, {"row": pair + cc, "col": zz * 2 + xl}

    mate = {"row": pair + 1 - core, "col": col}

    def z_side(s):
        return place(x, y, lax.rem(z + s + 8, 8), core)

    def xy_side(axis, s):
        if axis == 0:
            return place(lax.rem(x + s + 4, 4), y, z, core)
        return place(x, lax.rem(y + s + 4, 4), z, core)

    loads = [pltpu.make_async_copy(patt_hbm, patt, load_sem.at[0])]
    for i in range(2):
        for j in range(2):
            loads.append(pltpu.make_async_copy(dens.at[i, :, pl.ds(j * SIZE, SIZE)], blocks.at[i, j], load_sem.at[1 + 2 * i + j]))
    for load in loads:
        load.start()

    barrier = pltpu.get_barrier_semaphore()

    def greet(device):
        pl.semaphore_signal(barrier, 1, device_id=device, device_id_type=MESH)

    for d in range(GROUP):
        @pl.when(jnp.logical_or(d != col, jnp.logical_not(settled)))
        def _():
            greet({"row": part_xy, "col": d})

    for d in range(GROUP):
        @pl.when(jnp.logical_or(d != row, jnp.logical_not(settled)))
        def _():
            greet({"row": d, "col": part_z})

    for d in range(1, GROUP):
        greet(mate_target(d)[1])
    for axis in range(2):
        for s in (1, -1):
            greet(xy_side(axis, s))
    for load in loads:
        load.wait()
    pl.semaphore_wait(barrier, jnp.where(settled, 30, 32) + 19)

    lane = lax.broadcasted_iota(jnp.int32, (1, 128), 1)
    entries = jnp.zeros((1, 128), jnp.int32)
    for i in range(2):
        for j in range(2):
            entries = jnp.where(lane == i * 2 + j, patt[i, j], entries)
    pmsg[...] = entries

    def send(src, dst, send_sem, recv_sem, device):
        pltpu.make_async_remote_copy(src_ref=src, dst_ref=dst, send_sem=send_sem, recv_sem=recv_sem, device_id=device, device_id_type=MESH).start()

    def deliver(d, src, dst, send_sem, recv_sem, device, always_self):
        here = d == 0 if always_self else jnp.logical_and(d == 0, settled)

        @pl.when(here)
        def _():
            pltpu.make_async_copy(src, dst, recv_sem).start()

        @pl.when(jnp.logical_not(here))
        def _():
            send(src, dst, send_sem, recv_sem, device)

    def wait_for(ref, sem):
        pltpu.make_async_copy(ref, ref, sem).wait()

    def send_patterns(d, _):
        _, device = row_target(d)
        deliver(d, pmsg, prow.at[col], a2a_send.at[2], pat_recv.at[0], device, False)
        _, device = col_target(d)
        deliver(d, pmsg, pcol.at[row], a2a_send.at[2], pat_recv.at[1], device, False)
        return 0

    lax.fori_loop(0, GROUP, send_patterns, 0)

    def half(h):
        return pl.ds(h * HALF, HALF)

    def send_rows(c):
        def body(n, _):
            d = lax.rem(n + 7, GROUP)
            s, device = row_target(d)
            deliver(d, blocks.at[c // 2, :, pl.ds(pl.multiple_of(s * PART, PART), PART), half(c % 2)], rrecv[c].at[pl.ds(2 * col, 2)], a2a_send.at[0], row_recv.at[c], device, False)
            return 0

        lax.fori_loop(0, GROUP, body, 0)

    def send_columns(n, _):
        d = lax.rem(n + 7, GROUP)
        q, device = col_target(d)
        deliver(d, dens.at[:, pl.ds(pl.multiple_of(q * PART, PART), PART)], crecv.at[pl.ds(2 * row, 2)], a2a_send.at[1], col_recv, device, False)
        return 0

    send_rows(0)
    lax.fori_loop(0, GROUP, send_columns, 0)
    for c in range(1, 4):
        send_rows(c)

    for received in (*rrecv, *srecv):
        received[NB] = jnp.zeros((PART, HALF), BF16)
    crecv[NB] = jnp.zeros((PART, 2 * SIZE), BF16)
    for j in range(4):
        cpanel[j][:, SLOTS] = jnp.zeros((GROUP, PART, SIZE), BF16)

    wait_for(prow, pat_recv.at[0])
    wait_for(pcol, pat_recv.at[1])
    send(pcol, pmate, share_send.at[4], share_recv.at[4], mate)
    to_smem = [pltpu.make_async_copy(prow, prow_s, pat_copy.at[0]), pltpu.make_async_copy(pcol, pcol_s, pat_copy.at[1])]
    for c in to_smem:
        c.start()
    for c in to_smem:
        c.wait()

    def occupied(q, k):
        if q < 2:
            return prow_s[lax.div(k, 2), 0, q * 2 + lax.rem(k, 2)]
        return pcol_s[lax.div(k, 2), 0, lax.rem(k, 2) * 2 + (q - 2)]

    def backward(n, carry):
        k = NB - 1 - n
        later = []
        for q in range(4):
            nxt[q, k] = carry[q]
            later.append(carry[q] + occupied(q, k) * (k - carry[q]))
        return tuple(later)

    for q in range(4):
        nxt[q, NB] = NB
    first = lax.fori_loop(0, NB, backward, (jnp.int32(NB),) * 4)

    def forward(t, carry):
        later = []
        for q in range(4):
            idx[q, t] = carry[q]
            later.append(nxt[q, carry[q]])
        return tuple(later)

    lax.fori_loop(0, SLOTS, forward, first)

    def ranks(group, table):
        def count(k, carry):
            later = []
            for j in range(2):
                is_on = table[lax.div(k, 2), 0, lax.rem(k, 2) * 2 + j]
                rank[2 * group + j, k] = SLOTS + is_on * (carry[j] - SLOTS)
                later.append(carry[j] + is_on)
            return tuple(later)

        for j in range(2):
            rank[2 * group + j, NB] = SLOTS
        lax.fori_loop(0, NB, count, (jnp.int32(0),) * 2)

    ranks(0, pcol_s)

    def unit(j, da, db):
        dx, dy = (da, db) if j == 0 else (db, da)
        return lax.rem(y + dy + 4, 4) * 4 + lax.rem(x + dx + 4, 4)

    order = {0: 0, -1: 1, 1: 2, 2: 3}

    def column_send(j, q, half, axis, s, n):
        slots = pl.ds(0, SLOTS) if half is None else pl.ds(half * (SLOTS // 2), SLOTS // 2)
        ref = cpanel[j].at[q, slots]
        send(ref, ref, c_send.at[j], c_recv.at[j, n], xy_side(axis, s))

    def column_wait(j, q, half, n):
        slots = pl.ds(0, SLOTS) if half is None else pl.ds(half * (SLOTS // 2), SLOTS // 2)
        wait_for(cpanel[j].at[q, slots], c_recv.at[j, n])

    def column_along(j, da):
        for way, s in enumerate((1, -1)):
            column_send(j, unit(j, da, 0), None, 1 - j, s, 4 + order[da] * 2 + way)

    def column_own(j):
        def body(t, _):
            cpanel[j][part_xy, t] = crecv[idx[2 + j, t], :, j * SIZE : (j + 1) * SIZE]
            return 0

        lax.fori_loop(0, SLOTS, body, 0)

    def column_start():
        wait_for(crecv.at[pl.ds(0, NB)], col_recv)
        for j in range(2):
            column_own(j)
            for way, s in enumerate((1, -1)):
                column_send(j, unit(j, 0, 0), None, j, s, way)
        for j in range(2):
            column_along(j, 0)

    def column_near(j, s):
        way = (1 - s) // 2
        column_wait(j, unit(j, -s, 0), None, way)
        column_send(j, unit(j, -s, 0), way, j, s, 2 + way)
        column_along(j, -s)

    def column_far(j):
        for way in range(2):
            column_wait(j, unit(j, 2, 0), way, 2 + way)
        column_along(j, 2)

    def column_second(j, da, s):
        column_wait(j, unit(j, da, -s), None, 4 + order[da] * 2 + (1 - s) // 2)
        if (da in (0, -1)) == (s == 1):
            column_send(j, unit(j, da, -s), None, 1 - j, s, 12 + order[da])

    def column_last(j):
        for da in order:
            column_wait(j, unit(j, da, 2), None, 12 + order[da])
        ref = pl.ds(0, SLOTS)
        send(cpanel[j].at[:, ref], cpanel[2 + j].at[:, ref], share_send.at[j], share_recv.at[j], mate)

    def shared_panels():
        wait_for(pmate, share_recv.at[4])
        copy = pltpu.make_async_copy(pmate, pmate_s, pat_copy.at[0])
        copy.start()
        copy.wait()
        ranks(1, pmate_s)
        for j in range(2):
            wait_for(cpanel[2 + j].at[:, pl.ds(0, SLOTS)], share_recv.at[j])

    def slices(stage, c, d, part=None):
        zz = lax.rem(z + d + 8, 8)
        here = panel.at[c, zz * 2 + core] if stage == 0 else square_panel.at[c, zz]
        return here if part is None else here.at[:, pl.ds(part * (SLOTS // 2 * HALF), SLOTS // 2 * HALF)]

    def ring_send(stage, c, d, s, part=None):
        ref = slices(stage, c, -s * d, part)
        send(ref, ref, z_send.at[stage, c], z_recv.at[stage, c, (1 - s) // 2, d], z_side(s))

    def to_mate(stage, c, d):
        if stage == 0:
            ref = slices(stage, c, d)
            send(ref, ref, z_send.at[stage, c], mate_recv.at[c], mate)

    def ring_start(stage, c):
        received = (rrecv, srecv)[stage][c]
        wait_for(received.at[pl.ds(0, NB)], (row_recv, s_recv)[stage].at[c])

        def body(t, _):
            lanes = pl.ds(pl.multiple_of(t * HALF, HALF), HALF)
            if stage == 0:
                panel[c, part_z, :, lanes] = received[idx[c // 2, t]]
            else:
                square_panel[c, z, :, lanes] = received[idx[c // 2, t]]
            return 0

        lax.fori_loop(0, SLOTS, body, 0)
        for s in (1, -1):
            ring_send(stage, c, 0, s)
        to_mate(stage, c, 0)

    def ring_hop(stage, c, d):
        for way, s in enumerate((1, -1)):
            wait_for(slices(stage, c, -s * d), z_recv.at[stage, c, way, d - 1])
            ring_send(stage, c, d, s, None if d < 3 else way)
        for s in (1, -1):
            to_mate(stage, c, -s * d)

    def ring_last(stage, c):
        for way in range(2):
            wait_for(slices(stage, c, 4, way), z_recv.at[stage, c, way, 3])
        to_mate(stage, c, 4)

    def gather_rhs(i, group):
        def body(t, _):
            k = idx[i, t]
            for j in (2 * group, 2 * group + 1):
                slot = rank[j, k]
                for h in range(2):
                    block = cpanel[j][h * 8 : h * 8 + 8, slot]
                    rhs[2 * i + h, pl.ds(pl.multiple_of(t * HALF, HALF), HALF), j * SIZE : (j + 1) * SIZE] = block.reshape(HALF, SIZE)
            return 0

        lax.fori_loop(0, SLOTS, body, 0)

    def keep(i, j):
        group = core if j < 2 else 1 - core
        return prow_s[z * 2 + group, 0, i * 2 + j % 2].astype(F32)

    def square(c):
        i = c // 2
        wait_for(panel.at[c, pl.ds(0, 8)], mate_recv.at[c])
        value = jnp.dot(panel[c].reshape(SIZE, SLOTS * HALF), rhs[c, :, : 2 * SIZE], preferred_element_type=F32)
        if c % 2 == 0:
            sf[i] = value.reshape(8, 2, PART, 2 * SIZE)
            return
        value = sf[i].reshape(SIZE, 2 * SIZE) + value
        for j in range(2):
            kept = value[:, j * SIZE : (j + 1) * SIZE] * keep(i, j)
            sf[i, :, :, :, j * SIZE : (j + 1) * SIZE] = kept.reshape(8, 2, PART, SIZE)
            sl[i, j] = kept.astype(BF16)
        for h in range(2):
            def body(n, _):
                d = lax.rem(n + 7, GROUP)
                s, device = mate_target(d)
                deliver(d, sl.at[i, :, pl.ds(pl.multiple_of(s * PART, PART), PART), half(h)], srecv[2 * i + h].at[pl.ds(2 * part_z, 2)], s_send.at[i], s_recv.at[2 * i + h], device, True)
                return 0

            lax.fori_loop(0, GROUP, body, 0)
        send(sf.at[i, :, 1 - core], smate.at[i], share_send.at[2 + i], share_recv.at[2 + i], mate)

    def cube(c):
        i = c // 2
        value = jnp.dot(square_panel[c].reshape(HALF, SLOTS * HALF), rhs[c], preferred_element_type=F32)
        if c % 2 == 0:
            cf[i] = value
            return
        wait_for(smate.at[i], share_recv.at[2 + i])
        value = cf[i] + value
        value = jnp.concatenate([value[:, j * SIZE : (j + 1) * SIZE] * keep(i, j) for j in range(4)], axis=1).reshape(8, PART, 4 * SIZE)
        own = (3.0 * sf[i, :, core] - 2.0 * value[:, :, : 2 * SIZE]).astype(BF16)
        other = (3.0 * smate[i] - 2.0 * value[:, :, 2 * SIZE :]).astype(BF16)
        obuf[i, 1] = other

        @pl.when(settled)
        def _():
            send(obuf.at[i, 1], out.at[i, :, core], out_send, out_recv.at[i, core], {"row": row, "col": z * 2 + 1 - xl})
            out[i, :, core] = own

        @pl.when(jnp.logical_not(settled))
        def _():
            obuf[i, 0] = own
            send(obuf.at[i, 0], out.at[i, :, core], out_send, out_recv.at[i, core], {"row": pair + xl, "col": part_z})
            send(obuf.at[i, 1], out.at[i, :, core], out_send, out_recv.at[i, core], mate)

    ring_start(0, 0)
    column_start()
    ring_start(0, 1)
    ring_start(0, 2)
    column_near(0, 1)
    column_near(0, -1)
    ring_hop(0, 0, 1)
    column_near(1, 1)
    column_near(1, -1)
    ring_hop(0, 1, 1)
    ring_start(0, 3)
    ring_hop(0, 2, 1)
    column_second(1, 0, 1)
    ring_hop(0, 0, 2)
    column_second(1, 0, -1)
    column_second(0, 0, 1)
    column_second(0, 0, -1)
    ring_hop(0, 1, 2)
    column_far(0)
    column_second(0, -1, 1)
    ring_hop(0, 3, 1)
    column_second(0, -1, -1)
    column_second(1, -1, 1)
    column_second(1, -1, -1)
    column_second(0, 1, 1)
    ring_hop(0, 2, 2)
    column_second(0, 1, -1)
    column_second(1, 1, 1)
    column_second(1, 1, -1)
    ring_hop(0, 0, 3)
    column_far(1)
    ring_hop(0, 1, 3)
    column_second(0, 2, -1)
    ring_hop(0, 3, 2)
    ring_hop(0, 2, 3)
    ring_last(0, 0)
    column_second(0, 2, 1)
    ring_last(0, 1)
    ring_hop(0, 3, 3)
    ring_last(0, 2)
    column_second(1, 2, 1)
    column_second(1, 2, -1)
    column_last(0)
    ring_last(0, 3)
    column_last(1)
    gather_rhs(0, 0)
    square(0)
    square(1)
    gather_rhs(1, 0)
    square(2)
    square(3)
    ring_start(1, 0)
    ring_start(1, 1)
    shared_panels()
    gather_rhs(0, 1)
    ring_start(1, 2)
    gather_rhs(1, 1)
    ring_start(1, 3)
    ring_hop(1, 0, 1)
    ring_hop(1, 1, 1)
    ring_hop(1, 2, 1)
    ring_hop(1, 3, 1)
    ring_hop(1, 0, 2)
    ring_hop(1, 1, 2)
    ring_hop(1, 2, 2)
    ring_hop(1, 3, 2)
    ring_hop(1, 0, 3)
    ring_hop(1, 1, 3)
    ring_hop(1, 2, 3)
    ring_hop(1, 3, 3)
    ring_last(1, 0)
    ring_last(1, 1)
    cube(0)
    cube(1)
    ring_last(1, 2)
    ring_last(1, 3)
    cube(2)
    cube(3)

    for i in range(2):
        wait_for(out.at[i, :, 1 - core], out_recv.at[i, 1 - core])

    @pl.when(jnp.logical_not(settled))
    def _():
        for i in range(2):
            wait_for(out.at[i, :, core], out_recv.at[i, core])
            wait_for(obuf.at[i, 0], out_send)
        for c in range(4):
            wait_for(rrecv[c].at[pl.ds(0, 2)], a2a_send.at[0])
        wait_for(crecv.at[pl.ds(0, 2)], a2a_send.at[1])
        wait_for(prow.at[0], a2a_send.at[2])
        wait_for(pcol.at[0], a2a_send.at[2])

    for c in range(4):
        wait_for(rrecv[c].at[pl.ds(0, 30)], a2a_send.at[0])
    wait_for(crecv.at[pl.ds(0, 30)], a2a_send.at[1])
    wait_for(prow.at[pl.ds(1, 15)], a2a_send.at[2])
    wait_for(pcol.at[pl.ds(1, 15)], a2a_send.at[2])
    for i in range(2):
        wait_for(obuf.at[i, 1], out_send)
        wait_for(smate.at[i], share_send.at[2 + i])
    for c in range(4):
        wait_for(srecv[c].at[pl.ds(0, 30)], s_send.at[c // 2])
        wait_for(panel.at[c, pl.ds(0, 15)], z_send.at[0, c])
        wait_for(square_panel.at[c, pl.ds(0, 7)], z_send.at[1, c])
    wait_for(pcol, share_send.at[4])
    for j in range(2):
        wait_for(cpanel[j].at[:, pl.ds(0, SLOTS)], share_send.at[j])
        wait_for(cpanel[j].at[pl.ds(0, 15), pl.ds(0, SLOTS)], c_send.at[j])


def shards(density, pattern):
    vmem, smem, dma = pltpu.VMEM, pltpu.SMEM, pltpu.SemaphoreType.DMA
    received = [vmem((NB + 1, PART, HALF), BF16)] * 4
    panel = vmem((GROUP, SLOTS + 1, PART, SIZE), BF16)
    purified = pl.pallas_call(
        kernel,
        out_shape=jax.ShapeDtypeStruct((2, 8, 2, PART, 2 * SIZE), BF16),
        in_specs=[pl.BlockSpec(memory_space=pl.ANY)] * 2,
        out_specs=pl.BlockSpec(memory_space=vmem),
        scratch_shapes=[
            vmem((2, 2, SIZE, SIZE), BF16),
            smem((2, 2), jnp.int32),
            *received, *received,
            vmem((NB + 1, PART, 2 * SIZE), BF16),
            vmem((4, GROUP, PART, SLOTS * HALF), BF16),
            vmem((4, 8, PART, SLOTS * HALF), BF16),
            panel, panel, panel, panel,
            vmem((4, SLOTS * HALF, 4 * SIZE), BF16),
            vmem((2, 8, 2, PART, 2 * SIZE), F32),
            vmem((2, 8, PART, 2 * SIZE), F32),
            vmem((2, HALF, 4 * SIZE), F32),
            vmem((2, 2, SIZE, SIZE), BF16),
            vmem((2, 2, 8, PART, 2 * SIZE), BF16),
            vmem((1, 128), jnp.int32),
            vmem((GROUP, 1, 128), jnp.int32),
            vmem((GROUP, 1, 128), jnp.int32),
            vmem((GROUP, 1, 128), jnp.int32),
            smem((GROUP, 1, 128), jnp.int32),
            smem((GROUP, 1, 128), jnp.int32),
            smem((GROUP, 1, 128), jnp.int32),
            smem((4, NB + 1), jnp.int32),
            smem((4, SLOTS), jnp.int32),
            smem((4, NB + 1), jnp.int32),
            dma((5,)), dma((3,)), dma((4,)), dma, dma((2,)), dma((2,)),
            dma((2,)), dma((4,)), dma((2, 4)), dma((2, 4, 2, 4)), dma((4,)), dma((5,)), dma((5,)),
            dma((2,)), dma((2, 16)), dma, dma((2, 2)),
        ],
        compiler_params=pltpu.CompilerParams(collective_id=0, has_side_effects=True, vmem_limit_bytes=48 * 2**20),
        name="purify",
    )(density.reshape(2, SIZE, 2 * SIZE), pattern)
    return purified.reshape(2 * SIZE, 2 * SIZE)


def solution(mesh):
    return jax.shard_map(
        shards,
        mesh=mesh,
        in_specs=(P("row", "col"), P("row", "col")),
        out_specs=P("row", "col"),
        check_vma=False,
    )
```

```python
import functools

import jax
import jax.numpy as jnp
from jax import lax
from jax.experimental import pallas as pl
from jax.experimental.pallas import tpu as pltpu
from jax.sharding import PartitionSpec as P

MESH = pl.DeviceIdType.MESH
BF16 = jnp.bfloat16
F32 = jnp.float32
SIZE = 256
SLOTS = 12
HALF = SIZE // 2
NB = 32
GROUP = 16
PART = SIZE // GROUP


def place(x, y, z, core):
    return {"row": (y * 2 + lax.div(x, 2)) * 2 + core, "col": z * 2 + lax.rem(x, 2)}


def kernel(dens, patt_hbm, out, blocks, patt, rr0, rr1, rr2, rr3, sr0, sr1, sr2, sr3, crecv, panel, square_panel, cp0, cp1, cp2, cp3, rhs, sf, final, sl, obuf, pmsg, prow, pcol, pmate, prow_s, pcol_s, pmate_s, nxt, idx, rank, load_sem, a2a_send, row_recv, col_recv, pat_recv, pat_copy, s_send, s_recv, z_send, z_recv, mate_recv, share_send, share_recv, c_send, c_recv, out_send, out_recv):
    rrecv, srecv, cpanel = (rr0, rr1, rr2, rr3), (sr0, sr1, sr2, sr3), (cp0, cp1, cp2, cp3)
    row, col = lax.axis_index("row"), lax.axis_index("col")
    y, xh, core = lax.div(row, 4), lax.rem(lax.div(row, 2), 2), lax.rem(row, 2)
    z, xl = lax.div(col, 2), lax.rem(col, 2)
    x = xh * 2 + xl
    pair = (y * 2 + xh) * 2
    part_z = z * 2 + core
    part_xy = y * 4 + x
    settled = xl == core

    def row_target(d):
        zz, cc = lax.rem(z + lax.div(d, 2), 8), lax.rem(core + d, 2)
        return zz * 2 + cc, {"row": pair + cc, "col": zz * 2 + core}

    def col_target(d):
        q = lax.rem(part_xy + d, GROUP)
        return q, {"row": lax.div(q, 2) * 2 + xl, "col": z * 2 + lax.rem(q, 2)}

    def mate_target(d):
        zz, cc = lax.rem(z + lax.div(d, 2), 8), lax.rem(core + d, 2)
        return zz * 2 + cc, {"row": pair + cc, "col": zz * 2 + xl}

    mate = {"row": pair + 1 - core, "col": col}

    def z_side(s):
        return place(x, y, lax.rem(z + s + 8, 8), core)

    def xy_side(axis, s):
        if axis == 0:
            return place(lax.rem(x + s + 4, 4), y, z, core)
        return place(x, lax.rem(y + s + 4, 4), z, core)

    loads = [pltpu.make_async_copy(patt_hbm, patt, load_sem.at[0])]
    for i in range(2):
        for j in range(2):
            loads.append(pltpu.make_async_copy(dens.at[i, :, pl.ds(j * SIZE, SIZE)], blocks.at[i, j], load_sem.at[1 + 2 * i + j]))
    for load in loads:
        load.start()

    barrier = pltpu.get_barrier_semaphore()

    def greet(device):
        pl.semaphore_signal(barrier, 1, device_id=device, device_id_type=MESH)

    for d in range(GROUP):
        @pl.when(jnp.logical_or(d != col, jnp.logical_not(settled)))
        def _():
            greet({"row": part_xy, "col": d})

    for d in range(GROUP):
        @pl.when(jnp.logical_or(d != row, jnp.logical_not(settled)))
        def _():
            greet({"row": d, "col": part_z})

    for d in range(1, GROUP):
        greet(mate_target(d)[1])
    for axis in range(2):
        for s in (1, -1):
            greet(xy_side(axis, s))
    for load in loads:
        load.wait()
    pl.semaphore_wait(barrier, jnp.where(settled, 30, 32) + 19)

    lane = lax.broadcasted_iota(jnp.int32, (1, 128), 1)
    entries = jnp.zeros((1, 128), jnp.int32)
    for i in range(2):
        for j in range(2):
            entries = jnp.where(lane == i * 2 + j, patt[i, j], entries)
    pmsg[...] = entries

    def send(src, dst, send_sem, recv_sem, device):
        pltpu.make_async_remote_copy(src_ref=src, dst_ref=dst, send_sem=send_sem, recv_sem=recv_sem, device_id=device, device_id_type=MESH).start()

    def deliver(d, src, dst, send_sem, recv_sem, device, always_self):
        here = d == 0 if always_self else jnp.logical_and(d == 0, settled)

        @pl.when(here)
        def _():
            pltpu.make_async_copy(src, dst, recv_sem).start()

        @pl.when(jnp.logical_not(here))
        def _():
            send(src, dst, send_sem, recv_sem, device)

    def wait_for(ref, sem):
        pltpu.make_async_copy(ref, ref, sem).wait()

    def send_patterns(d, _):
        _, device = row_target(d)
        deliver(d, pmsg, prow.at[col], a2a_send.at[2], pat_recv.at[0], device, False)
        _, device = col_target(d)
        deliver(d, pmsg, pcol.at[row], a2a_send.at[2], pat_recv.at[1], device, False)
        return 0

    lax.fori_loop(0, GROUP, send_patterns, 0)

    def half(h):
        return pl.ds(h * HALF, HALF)

    def send_rows(c):
        def body(n, _):
            d = lax.rem(n + 7, GROUP)
            s, device = row_target(d)
            deliver(d, blocks.at[c // 2, :, pl.ds(pl.multiple_of(s * PART, PART), PART), half(c % 2)], rrecv[c].at[pl.ds(2 * col, 2)], a2a_send.at[0], row_recv.at[c], device, False)
            return 0

        lax.fori_loop(0, GROUP, body, 0)

    def send_columns(n, _):
        d = lax.rem(n + 7, GROUP)
        q, device = col_target(d)
        deliver(d, dens.at[:, pl.ds(pl.multiple_of(q * PART, PART), PART)], crecv.at[pl.ds(2 * row, 2)], a2a_send.at[1], col_recv, device, False)
        return 0

    send_rows(0)
    lax.fori_loop(0, GROUP, send_columns, 0)
    for c in range(1, 4):
        send_rows(c)

    for received in (*rrecv, *srecv):
        received[NB] = jnp.zeros((PART, HALF), BF16)
    crecv[NB] = jnp.zeros((PART, 2 * SIZE), BF16)
    for j in range(4):
        cpanel[j][:, SLOTS] = jnp.zeros((GROUP, PART, SIZE), BF16)

    wait_for(prow, pat_recv.at[0])
    wait_for(pcol, pat_recv.at[1])
    send(pcol, pmate, share_send.at[4], share_recv.at[4], mate)
    to_smem = [pltpu.make_async_copy(prow, prow_s, pat_copy.at[0]), pltpu.make_async_copy(pcol, pcol_s, pat_copy.at[1])]
    for c in to_smem:
        c.start()
    for c in to_smem:
        c.wait()

    def occupied(q, k):
        if q < 2:
            return prow_s[lax.div(k, 2), 0, q * 2 + lax.rem(k, 2)]
        return pcol_s[lax.div(k, 2), 0, lax.rem(k, 2) * 2 + (q - 2)]

    def backward(n, carry):
        k = NB - 1 - n
        later = []
        for q in range(4):
            nxt[q, k] = carry[q]
            later.append(carry[q] + occupied(q, k) * (k - carry[q]))
        return tuple(later)

    for q in range(4):
        nxt[q, NB] = NB
    first = lax.fori_loop(0, NB, backward, (jnp.int32(NB),) * 4)

    def forward(t, carry):
        later = []
        for q in range(4):
            idx[q, t] = carry[q]
            later.append(nxt[q, carry[q]])
        return tuple(later)

    lax.fori_loop(0, SLOTS, forward, first)

    def ranks(group, table):
        def count(k, carry):
            later = []
            for j in range(2):
                is_on = table[lax.div(k, 2), 0, lax.rem(k, 2) * 2 + j]
                rank[2 * group + j, k] = SLOTS + is_on * (carry[j] - SLOTS)
                later.append(carry[j] + is_on)
            return tuple(later)

        for j in range(2):
            rank[2 * group + j, NB] = SLOTS
        lax.fori_loop(0, NB, count, (jnp.int32(0),) * 2)

    ranks(0, pcol_s)

    def unit(j, da, db):
        dx, dy = (da, db) if j == 0 else (db, da)
        return lax.rem(y + dy + 4, 4) * 4 + lax.rem(x + dx + 4, 4)

    order = {0: 0, -1: 1, 1: 2, 2: 3}

    def column_send(j, q, half, axis, s, n):
        slots = pl.ds(0, SLOTS) if half is None else pl.ds(half * (SLOTS // 2), SLOTS // 2)
        ref = cpanel[j].at[q, slots]
        send(ref, ref, c_send.at[j], c_recv.at[j, n], xy_side(axis, s))

    def column_wait(j, q, half, n):
        slots = pl.ds(0, SLOTS) if half is None else pl.ds(half * (SLOTS // 2), SLOTS // 2)
        wait_for(cpanel[j].at[q, slots], c_recv.at[j, n])

    def column_along(j, da):
        for way, s in enumerate((1, -1)):
            column_send(j, unit(j, da, 0), None, 1 - j, s, 4 + order[da] * 2 + way)

    def column_own(j):
        def body(t, _):
            cpanel[j][part_xy, t] = crecv[idx[2 + j, t], :, j * SIZE : (j + 1) * SIZE]
            return 0

        lax.fori_loop(0, SLOTS, body, 0)

    def column_start():
        wait_for(crecv.at[pl.ds(0, NB)], col_recv)
        for j in range(2):
            column_own(j)
            for way, s in enumerate((1, -1)):
                column_send(j, unit(j, 0, 0), None, j, s, way)
        for j in range(2):
            column_along(j, 0)

    def column_near(j, s):
        way = (1 - s) // 2
        column_wait(j, unit(j, -s, 0), None, way)
        column_send(j, unit(j, -s, 0), way, j, s, 2 + way)
        column_along(j, -s)

    def column_far(j):
        for way in range(2):
            column_wait(j, unit(j, 2, 0), way, 2 + way)
        column_along(j, 2)

    def column_second(j, da, s):
        column_wait(j, unit(j, da, -s), None, 4 + order[da] * 2 + (1 - s) // 2)
        if (da in (0, -1)) == (s == 1):
            column_send(j, unit(j, da, -s), None, 1 - j, s, 12 + order[da])

    def column_last(j):
        for da in order:
            column_wait(j, unit(j, da, 2), None, 12 + order[da])
        ref = pl.ds(0, SLOTS)
        send(cpanel[j].at[:, ref], cpanel[2 + j].at[:, ref], share_send.at[j], share_recv.at[j], mate)

    def shared_panels():
        wait_for(pmate, share_recv.at[4])
        copy = pltpu.make_async_copy(pmate, pmate_s, pat_copy.at[0])
        copy.start()
        copy.wait()
        ranks(1, pmate_s)
        for j in range(2):
            wait_for(cpanel[2 + j].at[:, pl.ds(0, SLOTS)], share_recv.at[j])

    def slices(stage, c, d, part=None):
        zz = lax.rem(z + d + 8, 8)
        here = panel.at[c, zz * 2 + core] if stage == 0 else square_panel.at[c, zz]
        return here if part is None else here.at[:, pl.ds(part * (SLOTS // 2 * HALF), SLOTS // 2 * HALF)]

    def ring_send(stage, c, d, s, part=None):
        ref = slices(stage, c, -s * d, part)
        send(ref, ref, z_send.at[stage, c], z_recv.at[stage, c, (1 - s) // 2, d], z_side(s))

    def to_mate(stage, c, d, part=None):
        if stage == 0:
            ref = slices(stage, c, d, part)
            send(ref, ref, z_send.at[stage, c], mate_recv.at[c], mate)

    def ring_start(stage, c):
        received = (rrecv, srecv)[stage][c]
        wait_for(received.at[pl.ds(0, NB)], (row_recv, s_recv)[stage].at[c])

        def body(t, _):
            lanes = pl.ds(pl.multiple_of(t * HALF, HALF), HALF)
            if stage == 0:
                panel[c, part_z, :, lanes] = received[idx[c // 2, t]]
            else:
                square_panel[c, z, :, lanes] = received[idx[c // 2, t]]
            return 0

        lax.fori_loop(0, SLOTS, body, 0)
        for s in (1, -1):
            ring_send(stage, c, 0, s)
        to_mate(stage, c, 0)

    def ring_hop(stage, c, d):
        for way, s in enumerate((1, -1)):
            wait_for(slices(stage, c, -s * d), z_recv.at[stage, c, way, d - 1])
            ring_send(stage, c, d, s, None if d < 3 else way)
        for s in (1, -1):
            to_mate(stage, c, -s * d)

    def ring_last(stage, c):
        for way in range(2):
            wait_for(slices(stage, c, 4, way), z_recv.at[stage, c, way, 3])
            to_mate(stage, c, 4, way)

    def gather_rhs(i, group):
        def body(t, _):
            k = idx[i, t]
            for j in (2 * group, 2 * group + 1):
                slot = rank[j, k]
                for h in range(2):
                    block = cpanel[j][h * 8 : h * 8 + 8, slot]
                    rhs[2 * i + h, pl.ds(pl.multiple_of(t * HALF, HALF), HALF), j * SIZE : (j + 1) * SIZE] = block.reshape(HALF, SIZE)
            return 0

        lax.fori_loop(0, SLOTS, body, 0)

    def keep(i, j):
        group = core if j < 2 else 1 - core
        return prow_s[z * 2 + group, 0, i * 2 + j % 2].astype(F32)

    def square(c):
        i = c // 2
        wait_for(panel.at[c, pl.ds(0, 8)], mate_recv.at[c])
        value = jnp.dot(panel[c].reshape(SIZE, SLOTS * HALF), rhs[c, :, : 2 * SIZE], preferred_element_type=F32)
        if c % 2 == 0:
            sf[i] = value.reshape(8, 2, PART, 2 * SIZE)
            return
        value = sf[i].reshape(SIZE, 2 * SIZE) + value
        for j in range(2):
            kept = value[:, j * SIZE : (j + 1) * SIZE] * keep(i, j)
            sf[i, :, :, :, j * SIZE : (j + 1) * SIZE] = kept.reshape(8, 2, PART, SIZE)
            sl[i, j] = kept.astype(BF16)
        for h in range(2):
            def body(n, _):
                d = lax.rem(n + 7, GROUP)
                s, device = mate_target(d)
                deliver(d, sl.at[i, :, pl.ds(pl.multiple_of(s * PART, PART), PART), half(h)], srecv[2 * i + h].at[pl.ds(2 * part_z, 2)], s_send.at[i], s_recv.at[2 * i + h], device, True)
                return 0

            lax.fori_loop(0, GROUP, body, 0)
        send(sf.at[i, :, 1 - core], final.at[i, 1], share_send.at[2 + i], share_recv.at[2 + i], mate)

    def cube_rows(i, reach):
        here = [lax.rem(z + d + 8, 8) for d in reach]
        lhs = [jnp.concatenate([square_panel[c, zz] for zz in here], axis=0) for c in (2 * i, 2 * i + 1)]
        for step in range(2):
            group = jnp.where(settled, 1 - step, step)
            lanes = pl.ds(pl.multiple_of(group * 2 * SIZE, 2 * SIZE), 2 * SIZE)
            value = sum(jnp.dot(lhs[h], rhs[2 * i + h, :, lanes], preferred_element_type=F32) for h in range(2))
            holder = z * 2 + jnp.where(group == 0, core, 1 - core)
            kept = [value[:, j * SIZE : (j + 1) * SIZE] * prow_s[holder, 0, i * 2 + j].astype(F32) for j in range(2)]
            value = jnp.concatenate(kept, axis=1)
            done = []
            for n, zz in enumerate(here):
                done.append((3.0 * final[i, group, zz] - 2.0 * value[n * PART : (n + 1) * PART]).astype(BF16))
            if step == 0:
                for zz, rows in zip(here, done):
                    obuf[i, 0, zz] = rows
                    send(obuf.at[i, 0, zz], out.at[i, zz, core], out_send, out_recv.at[i, core], {"row": pair + xl, "col": z * 2 + 1 - xl})
                continue

            @pl.when(settled)
            def _():
                for zz, rows in zip(here, done):
                    out[i, zz, core] = rows

            @pl.when(jnp.logical_not(settled))
            def _():
                for zz, rows in zip(here, done):
                    obuf[i, 1, zz] = rows
                    send(obuf.at[i, 1, zz], out.at[i, zz, core], out_send, out_recv.at[i, core], mate)

    def cube_early(i):
        wait_for(final.at[i, 1], share_recv.at[2 + i])
        final[i, 0] = sf[i, :, core]
        cube_rows(i, (0, 1, -1, 2, -2))

    def cube_late(i):
        cube_rows(i, (3, -3, 4))

    ring_start(0, 0)
    column_start()
    ring_start(0, 1)
    ring_start(0, 2)
    column_near(0, 1)
    column_near(0, -1)
    ring_hop(0, 0, 1)
    column_near(1, 1)
    column_near(1, -1)
    ring_hop(0, 1, 1)
    ring_start(0, 3)
    ring_hop(0, 2, 1)
    column_second(1, 0, 1)
    ring_hop(0, 0, 2)
    column_second(1, 0, -1)
    column_second(0, 0, 1)
    column_second(0, 0, -1)
    ring_hop(0, 1, 2)
    column_far(0)
    column_second(0, -1, 1)
    ring_hop(0, 3, 1)
    column_second(0, -1, -1)
    column_second(1, -1, 1)
    column_second(1, -1, -1)
    column_second(0, 1, 1)
    ring_hop(0, 2, 2)
    column_second(0, 1, -1)
    column_second(1, 1, 1)
    column_second(1, 1, -1)
    ring_hop(0, 0, 3)
    column_far(1)
    ring_hop(0, 1, 3)
    column_second(0, 2, -1)
    ring_hop(0, 3, 2)
    ring_hop(0, 2, 3)
    ring_last(0, 0)
    column_second(0, 2, 1)
    ring_last(0, 1)
    ring_hop(0, 3, 3)
    ring_last(0, 2)
    column_second(1, 2, 1)
    column_second(1, 2, -1)
    column_last(0)
    ring_last(0, 3)
    column_last(1)
    gather_rhs(0, 0)
    square(0)
    square(1)
    gather_rhs(1, 0)
    square(2)
    square(3)
    ring_start(1, 0)
    ring_start(1, 1)
    shared_panels()
    gather_rhs(0, 1)
    ring_start(1, 2)
    gather_rhs(1, 1)
    ring_start(1, 3)
    ring_hop(1, 0, 1)
    ring_hop(1, 1, 1)
    ring_hop(1, 2, 1)
    ring_hop(1, 3, 1)
    ring_hop(1, 0, 2)
    ring_hop(1, 1, 2)
    ring_hop(1, 2, 2)
    ring_hop(1, 3, 2)
    cube_early(0)
    ring_hop(1, 0, 3)
    ring_hop(1, 1, 3)
    ring_hop(1, 2, 3)
    ring_hop(1, 3, 3)
    cube_early(1)
    ring_last(1, 0)
    ring_last(1, 1)
    cube_late(0)
    ring_last(1, 2)
    ring_last(1, 3)
    cube_late(1)

    for i in range(2):
        wait_for(out.at[i, :, 1 - core], out_recv.at[i, 1 - core])

    @pl.when(jnp.logical_not(settled))
    def _():
        for i in range(2):
            wait_for(out.at[i, :, core], out_recv.at[i, core])
            wait_for(obuf.at[i, 1], out_send)
        for c in range(4):
            wait_for(rrecv[c].at[pl.ds(0, 2)], a2a_send.at[0])
        wait_for(crecv.at[pl.ds(0, 2)], a2a_send.at[1])
        wait_for(prow.at[0], a2a_send.at[2])
        wait_for(pcol.at[0], a2a_send.at[2])

    for c in range(4):
        wait_for(rrecv[c].at[pl.ds(0, 30)], a2a_send.at[0])
    wait_for(crecv.at[pl.ds(0, 30)], a2a_send.at[1])
    wait_for(prow.at[pl.ds(1, 15)], a2a_send.at[2])
    wait_for(pcol.at[pl.ds(1, 15)], a2a_send.at[2])
    for i in range(2):
        wait_for(obuf.at[i, 0], out_send)
        wait_for(final.at[i, 1], share_send.at[2 + i])
    for c in range(4):
        wait_for(srecv[c].at[pl.ds(0, 30)], s_send.at[c // 2])
        wait_for(panel.at[c, pl.ds(0, 15)], z_send.at[0, c])
        wait_for(square_panel.at[c, pl.ds(0, 7)], z_send.at[1, c])
    wait_for(pcol, share_send.at[4])
    for j in range(2):
        wait_for(cpanel[j].at[:, pl.ds(0, SLOTS)], share_send.at[j])
        wait_for(cpanel[j].at[pl.ds(0, 15), pl.ds(0, SLOTS)], c_send.at[j])


def shards(density, pattern):
    vmem, smem, dma = pltpu.VMEM, pltpu.SMEM, pltpu.SemaphoreType.DMA
    received = [vmem((NB + 1, PART, HALF), BF16)] * 4
    panel = vmem((GROUP, SLOTS + 1, PART, SIZE), BF16)
    purified = pl.pallas_call(
        kernel,
        out_shape=jax.ShapeDtypeStruct((2, 8, 2, PART, 2 * SIZE), BF16),
        in_specs=[pl.BlockSpec(memory_space=pl.ANY)] * 2,
        out_specs=pl.BlockSpec(memory_space=vmem),
        scratch_shapes=[
            vmem((2, 2, SIZE, SIZE), BF16),
            smem((2, 2), jnp.int32),
            *received, *received,
            vmem((NB + 1, PART, 2 * SIZE), BF16),
            vmem((4, GROUP, PART, SLOTS * HALF), BF16),
            vmem((4, 8, PART, SLOTS * HALF), BF16),
            panel, panel, panel, panel,
            vmem((4, SLOTS * HALF, 4 * SIZE), BF16),
            vmem((2, 8, 2, PART, 2 * SIZE), F32),
            vmem((2, 2, 8, PART, 2 * SIZE), F32),
            vmem((2, 2, SIZE, SIZE), BF16),
            vmem((2, 2, 8, PART, 2 * SIZE), BF16),
            vmem((1, 128), jnp.int32),
            vmem((GROUP, 1, 128), jnp.int32),
            vmem((GROUP, 1, 128), jnp.int32),
            vmem((GROUP, 1, 128), jnp.int32),
            smem((GROUP, 1, 128), jnp.int32),
            smem((GROUP, 1, 128), jnp.int32),
            smem((GROUP, 1, 128), jnp.int32),
            smem((4, NB + 1), jnp.int32),
            smem((4, SLOTS), jnp.int32),
            smem((4, NB + 1), jnp.int32),
            dma((5,)), dma((3,)), dma((4,)), dma, dma((2,)), dma((2,)),
            dma((2,)), dma((4,)), dma((2, 4)), dma((2, 4, 2, 4)), dma((4,)), dma((5,)), dma((5,)),
            dma((2,)), dma((2, 16)), dma, dma((2, 2)),
        ],
        compiler_params=pltpu.CompilerParams(collective_id=0, has_side_effects=True, vmem_limit_bytes=48 * 2**20),
        name="purify",
    )(density.reshape(2, SIZE, 2 * SIZE), pattern)
    return purified.reshape(2 * SIZE, 2 * SIZE)


def solution(mesh):
    return jax.shard_map(
        shards,
        mesh=mesh,
        in_specs=(P("row", "col"), P("row", "col")),
        out_specs=P("row", "col"),
        check_vma=False,
    )
```

```python
import functools

import jax
import jax.numpy as jnp
from jax import lax
from jax.experimental import pallas as pl
from jax.experimental.pallas import tpu as pltpu
from jax.sharding import PartitionSpec as P

MESH = pl.DeviceIdType.MESH
BF16 = jnp.bfloat16
F32 = jnp.float32
SIZE = 256
SLOTS = 12
HALF = SIZE // 2
NB = 32
GROUP = 16
PART = SIZE // GROUP


def place(x, y, z, core):
    return {"row": (y * 2 + lax.div(x, 2)) * 2 + core, "col": z * 2 + lax.rem(x, 2)}


def kernel(dens, patt_hbm, out, blocks, patt, rr0, rr1, rr2, rr3, sr0, sr1, sr2, sr3, crecv, panel, square_panel, cp0, cp1, cp2, cp3, rhs, sf, final, sl, obuf, pmsg, prow, pcol, pmate, prow_s, pcol_s, pmate_s, nxt, idx, rank, load_sem, a2a_send, row_recv, col_recv, pat_recv, pat_copy, s_send, s_recv, z_send, z_recv, mate_recv, share_send, share_recv, c_send, c_recv, out_send, out_recv):
    rrecv, srecv, cpanel = (rr0, rr1, rr2, rr3), (sr0, sr1, sr2, sr3), (cp0, cp1, cp2, cp3)
    row, col = lax.axis_index("row"), lax.axis_index("col")
    y, xh, core = lax.div(row, 4), lax.rem(lax.div(row, 2), 2), lax.rem(row, 2)
    z, xl = lax.div(col, 2), lax.rem(col, 2)
    x = xh * 2 + xl
    pair = (y * 2 + xh) * 2
    part_z = z * 2 + core
    part_xy = y * 4 + x
    settled = xl == core

    def row_target(d):
        zz, cc = lax.rem(z + lax.div(d, 2), 8), lax.rem(core + d, 2)
        return zz * 2 + cc, {"row": pair + cc, "col": zz * 2 + core}

    def col_target(d):
        q = lax.rem(part_xy + d, GROUP)
        return q, {"row": lax.div(q, 2) * 2 + xl, "col": z * 2 + lax.rem(q, 2)}

    def mate_target(d):
        zz, cc = lax.rem(z + lax.div(d, 2), 8), lax.rem(core + d, 2)
        return zz * 2 + cc, {"row": pair + cc, "col": zz * 2 + xl}

    mate = {"row": pair + 1 - core, "col": col}

    def z_side(s):
        return place(x, y, lax.rem(z + s + 8, 8), core)

    def xy_side(axis, s):
        if axis == 0:
            return place(lax.rem(x + s + 4, 4), y, z, core)
        return place(x, lax.rem(y + s + 4, 4), z, core)

    loads = [pltpu.make_async_copy(patt_hbm, patt, load_sem.at[0])]
    for i in range(2):
        for j in range(2):
            loads.append(pltpu.make_async_copy(dens.at[i, :, pl.ds(j * SIZE, SIZE)], blocks.at[i, j], load_sem.at[1 + 2 * i + j]))
    for load in loads:
        load.start()

    barrier = pltpu.get_barrier_semaphore()

    def greet(device):
        pl.semaphore_signal(barrier, 1, device_id=device, device_id_type=MESH)

    for d in range(GROUP):
        @pl.when(jnp.logical_or(d != col, jnp.logical_not(settled)))
        def _():
            greet({"row": part_xy, "col": d})

    for d in range(GROUP):
        @pl.when(jnp.logical_or(d != row, jnp.logical_not(settled)))
        def _():
            greet({"row": d, "col": part_z})

    for d in range(1, GROUP):
        greet(mate_target(d)[1])
    for axis in range(2):
        for s in (1, -1):
            greet(xy_side(axis, s))
    for load in loads:
        load.wait()
    pl.semaphore_wait(barrier, jnp.where(settled, 30, 32) + 19)

    lane = lax.broadcasted_iota(jnp.int32, (1, 128), 1)
    entries = jnp.zeros((1, 128), jnp.int32)
    for i in range(2):
        for j in range(2):
            entries = jnp.where(lane == i * 2 + j, patt[i, j], entries)
    pmsg[...] = entries

    def send(src, dst, send_sem, recv_sem, device):
        pltpu.make_async_remote_copy(src_ref=src, dst_ref=dst, send_sem=send_sem, recv_sem=recv_sem, device_id=device, device_id_type=MESH).start()

    def deliver(d, src, dst, send_sem, recv_sem, device, always_self):
        here = d == 0 if always_self else jnp.logical_and(d == 0, settled)

        @pl.when(here)
        def _():
            pltpu.make_async_copy(src, dst, recv_sem).start()

        @pl.when(jnp.logical_not(here))
        def _():
            send(src, dst, send_sem, recv_sem, device)

    def wait_for(ref, sem):
        pltpu.make_async_copy(ref, ref, sem).wait()

    def send_patterns(d, _):
        _, device = row_target(d)
        deliver(d, pmsg, prow.at[col], a2a_send.at[2], pat_recv.at[0], device, False)
        _, device = col_target(d)
        deliver(d, pmsg, pcol.at[row], a2a_send.at[2], pat_recv.at[1], device, False)
        return 0

    lax.fori_loop(0, GROUP, send_patterns, 0)

    def half(h):
        return pl.ds(h * HALF, HALF)

    def send_rows(c):
        def body(n, _):
            d = lax.rem(n + 7, GROUP)
            s, device = row_target(d)
            deliver(d, blocks.at[c // 2, :, pl.ds(pl.multiple_of(s * PART, PART), PART), half(c % 2)], rrecv[c].at[pl.ds(2 * col, 2)], a2a_send.at[0], row_recv.at[c], device, False)
            return 0

        lax.fori_loop(0, GROUP, body, 0)

    def send_columns(n, _):
        d = lax.rem(n + 7, GROUP)
        q, device = col_target(d)
        deliver(d, dens.at[:, pl.ds(pl.multiple_of(q * PART, PART), PART)], crecv.at[pl.ds(2 * row, 2)], a2a_send.at[1], col_recv, device, False)
        return 0

    send_rows(0)
    lax.fori_loop(0, GROUP, send_columns, 0)
    for c in range(1, 4):
        send_rows(c)

    for received in (*rrecv, *srecv):
        received[NB] = jnp.zeros((PART, HALF), BF16)
    crecv[NB] = jnp.zeros((PART, 2 * SIZE), BF16)
    for j in range(4):
        cpanel[j][:, SLOTS] = jnp.zeros((GROUP, PART, SIZE), BF16)

    wait_for(prow, pat_recv.at[0])
    wait_for(pcol, pat_recv.at[1])
    send(pcol, pmate, share_send.at[4], share_recv.at[4], mate)
    to_smem = [pltpu.make_async_copy(prow, prow_s, pat_copy.at[0]), pltpu.make_async_copy(pcol, pcol_s, pat_copy.at[1])]
    for c in to_smem:
        c.start()
    for c in to_smem:
        c.wait()

    def occupied(q, k):
        if q < 2:
            return prow_s[lax.div(k, 2), 0, q * 2 + lax.rem(k, 2)]
        return pcol_s[lax.div(k, 2), 0, lax.rem(k, 2) * 2 + (q - 2)]

    def backward(n, carry):
        k = NB - 1 - n
        later = []
        for q in range(4):
            nxt[q, k] = carry[q]
            later.append(carry[q] + occupied(q, k) * (k - carry[q]))
        return tuple(later)

    for q in range(4):
        nxt[q, NB] = NB
    first = lax.fori_loop(0, NB, backward, (jnp.int32(NB),) * 4)

    def forward(t, carry):
        later = []
        for q in range(4):
            idx[q, t] = carry[q]
            later.append(nxt[q, carry[q]])
        return tuple(later)

    lax.fori_loop(0, SLOTS, forward, first)

    def ranks(group, table):
        def count(k, carry):
            later = []
            for j in range(2):
                is_on = table[lax.div(k, 2), 0, lax.rem(k, 2) * 2 + j]
                rank[2 * group + j, k] = SLOTS + is_on * (carry[j] - SLOTS)
                later.append(carry[j] + is_on)
            return tuple(later)

        for j in range(2):
            rank[2 * group + j, NB] = SLOTS
        lax.fori_loop(0, NB, count, (jnp.int32(0),) * 2)

    ranks(0, pcol_s)

    def unit(j, da, db):
        dx, dy = (da, db) if j == 0 else (db, da)
        return lax.rem(y + dy + 4, 4) * 4 + lax.rem(x + dx + 4, 4)

    order = {0: 0, -1: 1, 1: 2, 2: 3}

    def column_send(j, q, half, axis, s, n):
        slots = pl.ds(0, SLOTS) if half is None else pl.ds(half * (SLOTS // 2), SLOTS // 2)
        ref = cpanel[j].at[q, slots]
        send(ref, ref, c_send.at[j], c_recv.at[j, n], xy_side(axis, s))

    def column_wait(j, q, half, n):
        slots = pl.ds(0, SLOTS) if half is None else pl.ds(half * (SLOTS // 2), SLOTS // 2)
        wait_for(cpanel[j].at[q, slots], c_recv.at[j, n])

    def column_along(j, da):
        for way, s in enumerate((1, -1)):
            column_send(j, unit(j, da, 0), None, 1 - j, s, 4 + order[da] * 2 + way)

    def column_own(j):
        def body(t, _):
            cpanel[j][part_xy, t] = crecv[idx[2 + j, t], :, j * SIZE : (j + 1) * SIZE]
            return 0

        lax.fori_loop(0, SLOTS, body, 0)

    def column_start():
        wait_for(crecv.at[pl.ds(0, NB)], col_recv)
        for j in range(2):
            column_own(j)
            for way, s in enumerate((1, -1)):
                column_send(j, unit(j, 0, 0), None, j, s, way)
        for j in range(2):
            column_along(j, 0)

    def column_near(j, s):
        way = (1 - s) // 2
        column_wait(j, unit(j, -s, 0), None, way)
        column_send(j, unit(j, -s, 0), way, j, s, 2 + way)
        column_along(j, -s)

    def column_far(j):
        for way in range(2):
            column_wait(j, unit(j, 2, 0), way, 2 + way)
        column_along(j, 2)

    def column_second(j, da, s):
        column_wait(j, unit(j, da, -s), None, 4 + order[da] * 2 + (1 - s) // 2)
        if (da in (0, -1)) == (s == 1):
            column_send(j, unit(j, da, -s), None, 1 - j, s, 12 + order[da])

    def column_last(j):
        for da in order:
            column_wait(j, unit(j, da, 2), None, 12 + order[da])

    def share_panel(j):
        ref = pl.ds(0, SLOTS)
        send(cpanel[j].at[:, ref], cpanel[2 + j].at[:, ref], share_send.at[j], share_recv.at[j], mate)

    def shared_panels():
        wait_for(pmate, share_recv.at[4])
        copy = pltpu.make_async_copy(pmate, pmate_s, pat_copy.at[0])
        copy.start()
        copy.wait()
        ranks(1, pmate_s)
        for j in range(2):
            wait_for(cpanel[2 + j].at[:, pl.ds(0, SLOTS)], share_recv.at[j])

    def slices(stage, c, d, part=None):
        zz = lax.rem(z + d + 8, 8)
        here = panel.at[c, zz * 2 + core] if stage == 0 else square_panel.at[c, zz]
        return here if part is None else here.at[:, pl.ds(part * (SLOTS // 2 * HALF), SLOTS // 2 * HALF)]

    def ring_send(stage, c, d, s, part=None):
        ref = slices(stage, c, -s * d, part)
        send(ref, ref, z_send.at[stage, c], z_recv.at[stage, c, (1 - s) // 2, d], z_side(s))

    def to_mate(stage, c, d, part=None):
        if stage == 0:
            ref = slices(stage, c, d, part)
            send(ref, ref, z_send.at[stage, c], mate_recv.at[c], mate)

    def ring_start(stage, c):
        received = (rrecv, srecv)[stage][c]
        wait_for(received.at[pl.ds(0, NB)], (row_recv, s_recv)[stage].at[c])

        def body(t, _):
            lanes = pl.ds(pl.multiple_of(t * HALF, HALF), HALF)
            if stage == 0:
                panel[c, part_z, :, lanes] = received[idx[c // 2, t]]
            else:
                square_panel[c, z, :, lanes] = received[idx[c // 2, t]]
            return 0

        lax.fori_loop(0, SLOTS, body, 0)
        for s in (1, -1):
            ring_send(stage, c, 0, s)
        to_mate(stage, c, 0)

    def ring_hop(stage, c, d):
        for way, s in enumerate((1, -1)):
            wait_for(slices(stage, c, -s * d), z_recv.at[stage, c, way, d - 1])
            ring_send(stage, c, d, s, None if d < 3 else way)
        for s in (1, -1):
            to_mate(stage, c, -s * d)

    def ring_last(stage, c):
        for way in range(2):
            wait_for(slices(stage, c, 4, way), z_recv.at[stage, c, way, 3])
            to_mate(stage, c, 4, way)

    def gather_rhs(i, group):
        def body(t, _):
            k = idx[i, t]
            for j in (2 * group, 2 * group + 1):
                slot = rank[j, k]
                for h in range(2):
                    block = cpanel[j][h * 8 : h * 8 + 8, slot]
                    rhs[2 * i + h, pl.ds(pl.multiple_of(t * HALF, HALF), HALF), j * SIZE : (j + 1) * SIZE] = block.reshape(HALF, SIZE)
            return 0

        lax.fori_loop(0, SLOTS, body, 0)

    def keep(i, j):
        group = core if j < 2 else 1 - core
        return prow_s[z * 2 + group, 0, i * 2 + j % 2].astype(F32)

    def square(c):
        i = c // 2
        wait_for(panel.at[c, pl.ds(0, 8)], mate_recv.at[c])
        value = jnp.dot(panel[c].reshape(SIZE, SLOTS * HALF), rhs[c, :, : 2 * SIZE], preferred_element_type=F32)
        if c % 2 == 0:
            sf[i] = value.reshape(8, 2, PART, 2 * SIZE)
            return
        value = sf[i].reshape(SIZE, 2 * SIZE) + value
        for j in range(2):
            kept = value[:, j * SIZE : (j + 1) * SIZE] * keep(i, j)
            sf[i, :, :, :, j * SIZE : (j + 1) * SIZE] = kept.reshape(8, 2, PART, SIZE)
            sl[i, j] = kept.astype(BF16)
        for h in range(2):
            def body(n, _):
                d = lax.rem(n + 7, GROUP)
                s, device = mate_target(d)
                deliver(d, sl.at[i, :, pl.ds(pl.multiple_of(s * PART, PART), PART), half(h)], srecv[2 * i + h].at[pl.ds(2 * part_z, 2)], s_send.at[i], s_recv.at[2 * i + h], device, True)
                return 0

            lax.fori_loop(0, GROUP, body, 0)
        send(sf.at[i, :, 1 - core], final.at[i, 1], share_send.at[2 + i], share_recv.at[2 + i], mate)

    def cube_rows(i, reach):
        here = [lax.rem(z + d + 8, 8) for d in reach]
        lhs = [jnp.concatenate([square_panel[c, zz] for zz in here], axis=0) for c in (2 * i, 2 * i + 1)]
        for step in range(2):
            group = jnp.where(settled, 1 - step, step)
            lanes = pl.ds(pl.multiple_of(group * 2 * SIZE, 2 * SIZE), 2 * SIZE)
            value = sum(jnp.dot(lhs[h], rhs[2 * i + h, :, lanes], preferred_element_type=F32) for h in range(2))
            holder = z * 2 + jnp.where(group == 0, core, 1 - core)
            kept = [value[:, j * SIZE : (j + 1) * SIZE] * prow_s[holder, 0, i * 2 + j].astype(F32) for j in range(2)]
            value = jnp.concatenate(kept, axis=1)
            done = []
            for n, zz in enumerate(here):
                done.append((3.0 * final[i, group, zz] - 2.0 * value[n * PART : (n + 1) * PART]).astype(BF16))
            if step == 0:
                for zz, rows in zip(here, done):
                    obuf[i, 0, zz] = rows
                    send(obuf.at[i, 0, zz], out.at[i, zz, core], out_send, out_recv.at[i, core], {"row": pair + xl, "col": z * 2 + 1 - xl})
                continue

            @pl.when(settled)
            def _():
                for zz, rows in zip(here, done):
                    out[i, zz, core] = rows

            @pl.when(jnp.logical_not(settled))
            def _():
                for zz, rows in zip(here, done):
                    obuf[i, 1, zz] = rows
                    send(obuf.at[i, 1, zz], out.at[i, zz, core], out_send, out_recv.at[i, core], mate)

    def cube_early(i):
        wait_for(final.at[i, 1], share_recv.at[2 + i])
        final[i, 0] = sf[i, :, core]
        cube_rows(i, (0, 1, -1, 2, -2))

    def cube_late(i):
        cube_rows(i, (3, -3, 4))

    ring_start(0, 0)
    ring_start(0, 1)
    ring_start(0, 2)
    ring_hop(0, 0, 1)
    column_start()
    ring_hop(0, 1, 1)
    ring_start(0, 3)
    ring_hop(0, 2, 1)
    ring_hop(0, 0, 2)
    column_near(0, 1)
    ring_hop(0, 1, 2)
    column_near(0, -1)
    ring_hop(0, 3, 1)
    column_near(1, 1)
    column_near(1, -1)
    ring_hop(0, 2, 2)
    column_second(1, 0, 1)
    ring_hop(0, 0, 3)
    column_second(1, 0, -1)
    column_second(0, 0, 1)
    column_second(0, 0, -1)
    ring_hop(0, 1, 3)
    column_far(0)
    column_second(0, -1, 1)
    ring_hop(0, 3, 2)
    column_second(0, -1, -1)
    ring_hop(0, 2, 3)
    ring_last(0, 0)
    column_second(1, -1, 1)
    column_second(1, -1, -1)
    ring_last(0, 1)
    column_second(0, 1, 1)
    column_second(0, 1, -1)
    column_far(1)
    column_second(1, 1, 1)
    column_second(1, 1, -1)
    ring_hop(0, 3, 3)
    ring_last(0, 2)
    column_second(0, 2, -1)
    column_second(0, 2, 1)
    ring_last(0, 3)
    column_second(1, 2, -1)
    column_last(0)
    column_second(1, 2, 1)
    column_last(1)
    gather_rhs(0, 0)
    square(0)
    square(1)
    gather_rhs(1, 0)
    square(2)
    square(3)
    share_panel(0)
    share_panel(1)
    ring_start(1, 0)
    ring_start(1, 1)
    shared_panels()
    gather_rhs(0, 1)
    ring_start(1, 2)
    gather_rhs(1, 1)
    ring_start(1, 3)
    ring_hop(1, 0, 1)
    ring_hop(1, 1, 1)
    ring_hop(1, 2, 1)
    ring_hop(1, 3, 1)
    ring_hop(1, 0, 2)
    ring_hop(1, 1, 2)
    ring_hop(1, 2, 2)
    ring_hop(1, 3, 2)
    cube_early(0)
    ring_hop(1, 0, 3)
    ring_hop(1, 1, 3)
    ring_hop(1, 2, 3)
    ring_hop(1, 3, 3)
    cube_early(1)
    ring_last(1, 0)
    ring_last(1, 1)
    cube_late(0)
    ring_last(1, 2)
    ring_last(1, 3)
    cube_late(1)

    for i in range(2):
        wait_for(out.at[i, :, 1 - core], out_recv.at[i, 1 - core])

    @pl.when(jnp.logical_not(settled))
    def _():
        for i in range(2):
            wait_for(out.at[i, :, core], out_recv.at[i, core])
            wait_for(obuf.at[i, 1], out_send)
        for c in range(4):
            wait_for(rrecv[c].at[pl.ds(0, 2)], a2a_send.at[0])
        wait_for(crecv.at[pl.ds(0, 2)], a2a_send.at[1])
        wait_for(prow.at[0], a2a_send.at[2])
        wait_for(pcol.at[0], a2a_send.at[2])

    for c in range(4):
        wait_for(rrecv[c].at[pl.ds(0, 30)], a2a_send.at[0])
    wait_for(crecv.at[pl.ds(0, 30)], a2a_send.at[1])
    wait_for(prow.at[pl.ds(1, 15)], a2a_send.at[2])
    wait_for(pcol.at[pl.ds(1, 15)], a2a_send.at[2])
    for i in range(2):
        wait_for(obuf.at[i, 0], out_send)
        wait_for(final.at[i, 1], share_send.at[2 + i])
    for c in range(4):
        wait_for(srecv[c].at[pl.ds(0, 30)], s_send.at[c // 2])
        wait_for(panel.at[c, pl.ds(0, 15)], z_send.at[0, c])
        wait_for(square_panel.at[c, pl.ds(0, 7)], z_send.at[1, c])
    wait_for(pcol, share_send.at[4])
    for j in range(2):
        wait_for(cpanel[j].at[:, pl.ds(0, SLOTS)], share_send.at[j])
        wait_for(cpanel[j].at[pl.ds(0, 15), pl.ds(0, SLOTS)], c_send.at[j])


def shards(density, pattern):
    vmem, smem, dma = pltpu.VMEM, pltpu.SMEM, pltpu.SemaphoreType.DMA
    received = [vmem((NB + 1, PART, HALF), BF16)] * 4
    panel = vmem((GROUP, SLOTS + 1, PART, SIZE), BF16)
    purified = pl.pallas_call(
        kernel,
        out_shape=jax.ShapeDtypeStruct((2, 8, 2, PART, 2 * SIZE), BF16),
        in_specs=[pl.BlockSpec(memory_space=pl.ANY)] * 2,
        out_specs=pl.BlockSpec(memory_space=vmem),
        scratch_shapes=[
            vmem((2, 2, SIZE, SIZE), BF16),
            smem((2, 2), jnp.int32),
            *received, *received,
            vmem((NB + 1, PART, 2 * SIZE), BF16),
            vmem((4, GROUP, PART, SLOTS * HALF), BF16),
            vmem((4, 8, PART, SLOTS * HALF), BF16),
            panel, panel, panel, panel,
            vmem((4, SLOTS * HALF, 4 * SIZE), BF16),
            vmem((2, 8, 2, PART, 2 * SIZE), F32),
            vmem((2, 2, 8, PART, 2 * SIZE), F32),
            vmem((2, 2, SIZE, SIZE), BF16),
            vmem((2, 2, 8, PART, 2 * SIZE), BF16),
            vmem((1, 128), jnp.int32),
            vmem((GROUP, 1, 128), jnp.int32),
            vmem((GROUP, 1, 128), jnp.int32),
            vmem((GROUP, 1, 128), jnp.int32),
            smem((GROUP, 1, 128), jnp.int32),
            smem((GROUP, 1, 128), jnp.int32),
            smem((GROUP, 1, 128), jnp.int32),
            smem((4, NB + 1), jnp.int32),
            smem((4, SLOTS), jnp.int32),
            smem((4, NB + 1), jnp.int32),
            dma((5,)), dma((3,)), dma((4,)), dma, dma((2,)), dma((2,)),
            dma((2,)), dma((4,)), dma((2, 4)), dma((2, 4, 2, 4)), dma((4,)), dma((5,)), dma((5,)),
            dma((2,)), dma((2, 16)), dma, dma((2, 2)),
        ],
        compiler_params=pltpu.CompilerParams(collective_id=0, has_side_effects=True, vmem_limit_bytes=48 * 2**20),
        name="purify",
    )(density.reshape(2, SIZE, 2 * SIZE), pattern)
    return purified.reshape(2 * SIZE, 2 * SIZE)


def solution(mesh):
    return jax.shard_map(
        shards,
        mesh=mesh,
        in_specs=(P("row", "col"), P("row", "col")),
        out_specs=P("row", "col"),
        check_vma=False,
    )
```

```python
import functools

import jax
import jax.numpy as jnp
from jax import lax
from jax.experimental import pallas as pl
from jax.experimental.pallas import tpu as pltpu
from jax.sharding import PartitionSpec as P

MESH = pl.DeviceIdType.MESH
BF16 = jnp.bfloat16
F32 = jnp.float32
SIZE = 256
SLOTS = 12
HALF = SIZE // 2
NB = 32
GROUP = 16
PART = SIZE // GROUP


def place(x, y, z, core):
    return {"row": (y * 2 + lax.div(x, 2)) * 2 + core, "col": z * 2 + lax.rem(x, 2)}


def kernel(dens, patt_hbm, out, blocks, patt, rr0, rr1, rr2, rr3, sr0, sr1, sr2, sr3, crecv, panel, square_panel, cp0, cp1, cp2, cp3, rhs, sf, final, sl, obuf, pmsg, prow, pcol, pmate, prow_s, pcol_s, pmate_s, nxt, idx, rank, load_sem, a2a_send, row_recv, col_recv, pat_recv, pat_copy, s_send, s_recv, z_send, z_recv, mate_recv, share_send, share_recv, c_send, c_recv, out_send, out_recv):
    rrecv, srecv, cpanel = (rr0, rr1, rr2, rr3), (sr0, sr1, sr2, sr3), (cp0, cp1, cp2, cp3)
    row, col = lax.axis_index("row"), lax.axis_index("col")
    y, xh, core = lax.div(row, 4), lax.rem(lax.div(row, 2), 2), lax.rem(row, 2)
    z, xl = lax.div(col, 2), lax.rem(col, 2)
    x = xh * 2 + xl
    pair = (y * 2 + xh) * 2
    part_z = z * 2 + core
    part_xy = y * 4 + x
    settled = xl == core

    def row_target(d):
        zz, cc = lax.rem(z + lax.div(d, 2), 8), lax.rem(core + d, 2)
        return zz * 2 + cc, {"row": pair + cc, "col": zz * 2 + core}

    def col_target(d):
        q = lax.rem(part_xy + d, GROUP)
        return q, {"row": lax.div(q, 2) * 2 + xl, "col": z * 2 + lax.rem(q, 2)}

    def mate_target(d):
        zz, cc = lax.rem(z + lax.div(d, 2), 8), lax.rem(core + d, 2)
        return zz * 2 + cc, {"row": pair + cc, "col": zz * 2 + xl}

    mate = {"row": pair + 1 - core, "col": col}

    def z_side(s):
        return place(x, y, lax.rem(z + s + 8, 8), core)

    def xy_side(axis, s):
        if axis == 0:
            return place(lax.rem(x + s + 4, 4), y, z, core)
        return place(x, lax.rem(y + s + 4, 4), z, core)

    loads = [pltpu.make_async_copy(patt_hbm, patt, load_sem.at[0])]
    for i in range(2):
        for j in range(2):
            loads.append(pltpu.make_async_copy(dens.at[i, :, pl.ds(j * SIZE, SIZE)], blocks.at[i, j], load_sem.at[1 + 2 * i + j]))
    for load in loads:
        load.start()

    barrier = pltpu.get_barrier_semaphore()

    def greet(device):
        pl.semaphore_signal(barrier, 1, device_id=device, device_id_type=MESH)

    for d in range(GROUP):
        @pl.when(jnp.logical_or(d != col, jnp.logical_not(settled)))
        def _():
            greet({"row": part_xy, "col": d})

    for d in range(GROUP):
        @pl.when(jnp.logical_or(d != row, jnp.logical_not(settled)))
        def _():
            greet({"row": d, "col": part_z})

    for d in range(1, GROUP):
        greet(mate_target(d)[1])
    for axis in range(2):
        for s in (1, -1):
            greet(xy_side(axis, s))
    for load in loads:
        load.wait()
    pl.semaphore_wait(barrier, jnp.where(settled, 30, 32) + 19)

    lane = lax.broadcasted_iota(jnp.int32, (1, 128), 1)
    entries = jnp.zeros((1, 128), jnp.int32)
    for i in range(2):
        for j in range(2):
            entries = jnp.where(lane == i * 2 + j, patt[i, j], entries)
    pmsg[...] = entries

    def send(src, dst, send_sem, recv_sem, device):
        pltpu.make_async_remote_copy(src_ref=src, dst_ref=dst, send_sem=send_sem, recv_sem=recv_sem, device_id=device, device_id_type=MESH).start()

    def deliver(d, src, dst, send_sem, recv_sem, device, always_self):
        here = d == 0 if always_self else jnp.logical_and(d == 0, settled)

        @pl.when(here)
        def _():
            pltpu.make_async_copy(src, dst, recv_sem).start()

        @pl.when(jnp.logical_not(here))
        def _():
            send(src, dst, send_sem, recv_sem, device)

    def wait_for(ref, sem):
        pltpu.make_async_copy(ref, ref, sem).wait()

    def send_patterns(d, _):
        _, device = row_target(d)
        deliver(d, pmsg, prow.at[col], a2a_send.at[2], pat_recv.at[0], device, False)
        _, device = col_target(d)
        deliver(d, pmsg, pcol.at[row], a2a_send.at[2], pat_recv.at[1], device, False)
        return 0

    lax.fori_loop(0, GROUP, send_patterns, 0)

    def half(h):
        return pl.ds(h * HALF, HALF)

    def send_rows(c):
        def body(n, _):
            d = lax.rem(n + 7, GROUP)
            s, device = row_target(d)
            deliver(d, blocks.at[c // 2, :, pl.ds(pl.multiple_of(s * PART, PART), PART), half(c % 2)], rrecv[c].at[pl.ds(2 * col, 2)], a2a_send.at[0], row_recv.at[c], device, False)
            return 0

        lax.fori_loop(0, GROUP, body, 0)

    def send_columns(n, _):
        d = lax.rem(n + 7, GROUP)
        q, device = col_target(d)
        deliver(d, dens.at[:, pl.ds(pl.multiple_of(q * PART, PART), PART)], crecv.at[pl.ds(2 * row, 2)], a2a_send.at[1], col_recv, device, False)
        return 0

    send_rows(0)
    lax.fori_loop(0, GROUP, send_columns, 0)
    for c in range(1, 4):
        send_rows(c)

    for received in (*rrecv, *srecv):
        received[NB] = jnp.zeros((PART, HALF), BF16)
    crecv[NB] = jnp.zeros((PART, 2 * SIZE), BF16)
    for j in range(4):
        cpanel[j][:, SLOTS] = jnp.zeros((GROUP, PART, SIZE), BF16)

    wait_for(prow, pat_recv.at[0])
    wait_for(pcol, pat_recv.at[1])
    send(pcol, pmate, share_send.at[4], share_recv.at[4], mate)
    to_smem = [pltpu.make_async_copy(prow, prow_s, pat_copy.at[0]), pltpu.make_async_copy(pcol, pcol_s, pat_copy.at[1])]
    for c in to_smem:
        c.start()
    for c in to_smem:
        c.wait()

    def occupied(q, k):
        if q < 2:
            return prow_s[lax.div(k, 2), 0, q * 2 + lax.rem(k, 2)]
        return pcol_s[lax.div(k, 2), 0, lax.rem(k, 2) * 2 + (q - 2)]

    def backward(n, carry):
        k = NB - 1 - n
        later = []
        for q in range(4):
            nxt[q, k] = carry[q]
            later.append(carry[q] + occupied(q, k) * (k - carry[q]))
        return tuple(later)

    for q in range(4):
        nxt[q, NB] = NB
    first = lax.fori_loop(0, NB, backward, (jnp.int32(NB),) * 4)

    def forward(t, carry):
        later = []
        for q in range(4):
            idx[q, t] = carry[q]
            later.append(nxt[q, carry[q]])
        return tuple(later)

    lax.fori_loop(0, SLOTS, forward, first)

    def ranks(group, table):
        def count(k, carry):
            later = []
            for j in range(2):
                is_on = table[lax.div(k, 2), 0, lax.rem(k, 2) * 2 + j]
                rank[2 * group + j, k] = SLOTS + is_on * (carry[j] - SLOTS)
                later.append(carry[j] + is_on)
            return tuple(later)

        for j in range(2):
            rank[2 * group + j, NB] = SLOTS
        lax.fori_loop(0, NB, count, (jnp.int32(0),) * 2)

    ranks(0, pcol_s)

    def unit(j, da, db):
        dx, dy = (da, db) if j == 0 else (db, da)
        return lax.rem(y + dy + 4, 4) * 4 + lax.rem(x + dx + 4, 4)

    order = {0: 0, -1: 1, 1: 2, 2: 3}

    def column_send(j, q, half, axis, s, n):
        slots = pl.ds(0, SLOTS) if half is None else pl.ds(half * (SLOTS // 2), SLOTS // 2)
        ref = cpanel[j].at[q, slots]
        send(ref, ref, c_send.at[j], c_recv.at[j, n], xy_side(axis, s))

    def column_wait(j, q, half, n):
        slots = pl.ds(0, SLOTS) if half is None else pl.ds(half * (SLOTS // 2), SLOTS // 2)
        wait_for(cpanel[j].at[q, slots], c_recv.at[j, n])

    def column_along(j, da):
        for way, s in enumerate((1, -1)):
            column_send(j, unit(j, da, 0), None, 1 - j, s, 4 + order[da] * 2 + way)

    def column_own(j):
        def body(t, _):
            cpanel[j][part_xy, t] = crecv[idx[2 + j, t], :, j * SIZE : (j + 1) * SIZE]
            return 0

        lax.fori_loop(0, SLOTS, body, 0)

    def column_start():
        wait_for(crecv.at[pl.ds(0, NB)], col_recv)
        for j in range(2):
            column_own(j)
            for way, s in enumerate((1, -1)):
                column_send(j, unit(j, 0, 0), None, j, s, way)
        for j in range(2):
            column_along(j, 0)

    def column_near(j, s):
        way = (1 - s) // 2
        column_wait(j, unit(j, -s, 0), None, way)
        column_send(j, unit(j, -s, 0), way, j, s, 2 + way)
        column_along(j, -s)

    def column_far(j):
        for way in range(2):
            column_wait(j, unit(j, 2, 0), way, 2 + way)
        column_along(j, 2)

    def column_second(j, da, s):
        column_wait(j, unit(j, da, -s), None, 4 + order[da] * 2 + (1 - s) // 2)
        if (da in (0, -1)) == (s == 1):
            column_send(j, unit(j, da, -s), None, 1 - j, s, 12 + order[da])

    def column_last(j):
        for da in order:
            column_wait(j, unit(j, da, 2), None, 12 + order[da])

    def share_panel(j):
        ref = pl.ds(0, SLOTS)
        send(cpanel[j].at[:, ref], cpanel[2 + j].at[:, ref], share_send.at[j], share_recv.at[j], mate)

    def shared_panels():
        wait_for(pmate, share_recv.at[4])
        copy = pltpu.make_async_copy(pmate, pmate_s, pat_copy.at[0])
        copy.start()
        copy.wait()
        ranks(1, pmate_s)
        for j in range(2):
            wait_for(cpanel[2 + j].at[:, pl.ds(0, SLOTS)], share_recv.at[j])

    def slices(stage, c, d, part=None):
        zz = lax.rem(z + d + 8, 8)
        here = panel.at[c, zz * 2 + core] if stage == 0 else square_panel.at[c, zz]
        return here if part is None else here.at[:, pl.ds(part * (SLOTS // 2 * HALF), SLOTS // 2 * HALF)]

    def ring_send(stage, c, d, s, part=None):
        ref = slices(stage, c, -s * d, part)
        send(ref, ref, z_send.at[stage, c], z_recv.at[stage, c, (1 - s) // 2, d], z_side(s))

    def to_mate(stage, c, d, part=None):
        if stage == 0:
            ref = slices(stage, c, d, part)
            send(ref, ref, z_send.at[stage, c], mate_recv.at[c], mate)

    def ring_start(stage, c):
        received = (rrecv, srecv)[stage][c]
        wait_for(received.at[pl.ds(0, NB)], (row_recv, s_recv)[stage].at[c])

        def body(t, _):
            lanes = pl.ds(pl.multiple_of(t * HALF, HALF), HALF)
            if stage == 0:
                panel[c, part_z, :, lanes] = received[idx[c // 2, t]]
            else:
                square_panel[c, z, :, lanes] = received[idx[c // 2, t]]
            return 0

        lax.fori_loop(0, SLOTS, body, 0)
        for s in (1, -1):
            ring_send(stage, c, 0, s)
        to_mate(stage, c, 0)

    def ring_hop(stage, c, d):
        for way, s in enumerate((1, -1)):
            wait_for(slices(stage, c, -s * d), z_recv.at[stage, c, way, d - 1])
            ring_send(stage, c, d, s, None if d < 3 else way)
        for s in (1, -1):
            to_mate(stage, c, -s * d)

    def ring_last(stage, c):
        for way in range(2):
            wait_for(slices(stage, c, 4, way), z_recv.at[stage, c, way, 3])
            to_mate(stage, c, 4, way)

    def gather_rhs(i, group):
        def body(t, _):
            k = idx[i, t]
            for j in (2 * group, 2 * group + 1):
                slot = rank[j, k]
                for h in range(2):
                    block = cpanel[j][h * 8 : h * 8 + 8, slot]
                    rhs[2 * i + h, pl.ds(pl.multiple_of(t * HALF, HALF), HALF), j * SIZE : (j + 1) * SIZE] = block.reshape(HALF, SIZE)
            return 0

        lax.fori_loop(0, SLOTS, body, 0)

    def keep(i, j):
        group = core if j < 2 else 1 - core
        return prow_s[z * 2 + group, 0, i * 2 + j % 2].astype(F32)

    def square(c):
        i = c // 2
        wait_for(panel.at[c, pl.ds(0, 8)], mate_recv.at[c])
        value = jnp.dot(panel[c].reshape(SIZE, SLOTS * HALF), rhs[c, :, : 2 * SIZE], preferred_element_type=F32)
        if c % 2 == 0:
            sf[i] = value.reshape(8, 2, PART, 2 * SIZE)
            return
        value = sf[i].reshape(SIZE, 2 * SIZE) + value
        for j in range(2):
            kept = value[:, j * SIZE : (j + 1) * SIZE] * keep(i, j)
            sf[i, :, :, :, j * SIZE : (j + 1) * SIZE] = kept.reshape(8, 2, PART, SIZE)
            sl[i, j] = kept.astype(BF16)
        for h in range(2):
            def body(n, _):
                d = lax.rem(n + 7, GROUP)
                s, device = mate_target(d)
                deliver(d, sl.at[i, :, pl.ds(pl.multiple_of(s * PART, PART), PART), half(h)], srecv[2 * i + h].at[pl.ds(2 * part_z, 2)], s_send.at[i], s_recv.at[2 * i + h], device, True)
                return 0

            lax.fori_loop(0, GROUP, body, 0)
        send(sf.at[i, :, 1 - core], final.at[i, 1], share_send.at[2 + i], share_recv.at[2 + i], mate)

    def cube_rows(i, reach):
        here = [lax.rem(z + d + 8, 8) for d in reach]
        lhs = [jnp.concatenate([square_panel[c, zz] for zz in here], axis=0) for c in (2 * i, 2 * i + 1)]
        for step in range(2):
            group = jnp.where(settled, 1 - step, step)
            lanes = pl.ds(pl.multiple_of(group * 2 * SIZE, 2 * SIZE), 2 * SIZE)
            value = sum(jnp.dot(lhs[h], rhs[2 * i + h, :, lanes], preferred_element_type=F32) for h in range(2))
            holder = z * 2 + jnp.where(group == 0, core, 1 - core)
            kept = [value[:, j * SIZE : (j + 1) * SIZE] * prow_s[holder, 0, i * 2 + j].astype(F32) for j in range(2)]
            value = jnp.concatenate(kept, axis=1)
            done = []
            for n, zz in enumerate(here):
                done.append((3.0 * final[i, group, zz] - 2.0 * value[n * PART : (n + 1) * PART]).astype(BF16))
            if step == 0:
                for zz, rows in zip(here, done):
                    obuf[i, 0, zz] = rows
                    send(obuf.at[i, 0, zz], out.at[i, zz, core], out_send, out_recv.at[i, core], {"row": pair + xl, "col": z * 2 + 1 - xl})
                continue

            @pl.when(settled)
            def _():
                for zz, rows in zip(here, done):
                    out[i, zz, core] = rows

            @pl.when(jnp.logical_not(settled))
            def _():
                for zz, rows in zip(here, done):
                    obuf[i, 1, zz] = rows
                    send(obuf.at[i, 1, zz], out.at[i, zz, core], out_send, out_recv.at[i, core], mate)

    def cube_early(i):
        wait_for(final.at[i, 1], share_recv.at[2 + i])
        final[i, 0] = sf[i, :, core]
        cube_rows(i, (0, 1, -1, 2, -2))

    def cube_late(i):
        cube_rows(i, (3, -3, 4))

    ring_start(0, 0)
    column_start()
    ring_start(0, 1)
    ring_start(0, 2)
    column_near(0, 1)
    column_near(0, -1)
    ring_hop(0, 0, 1)
    column_near(1, 1)
    column_near(1, -1)
    ring_hop(0, 1, 1)
    ring_start(0, 3)
    ring_hop(0, 2, 1)
    column_second(1, 0, 1)
    ring_hop(0, 0, 2)
    column_second(1, 0, -1)
    column_second(0, 0, 1)
    column_second(0, 0, -1)
    ring_hop(0, 1, 2)
    column_far(0)
    column_second(0, -1, 1)
    ring_hop(0, 3, 1)
    column_second(0, -1, -1)
    column_second(1, -1, 1)
    column_second(1, -1, -1)
    column_second(0, 1, 1)
    ring_hop(0, 2, 2)
    column_second(0, 1, -1)
    column_second(1, 1, 1)
    column_second(1, 1, -1)
    ring_hop(0, 0, 3)
    column_far(1)
    ring_hop(0, 1, 3)
    column_second(0, 2, -1)
    ring_hop(0, 3, 2)
    ring_hop(0, 2, 3)
    ring_last(0, 0)
    column_second(0, 2, 1)
    ring_last(0, 1)
    ring_hop(0, 3, 3)
    ring_last(0, 2)
    column_second(1, 2, 1)
    column_second(1, 2, -1)
    column_last(0)
    ring_last(0, 3)
    column_last(1)
    gather_rhs(0, 0)
    square(0)
    square(1)
    gather_rhs(1, 0)
    square(2)
    square(3)
    share_panel(0)
    share_panel(1)
    ring_start(1, 0)
    ring_start(1, 1)
    shared_panels()
    gather_rhs(0, 1)
    ring_start(1, 2)
    gather_rhs(1, 1)
    ring_start(1, 3)
    ring_hop(1, 0, 1)
    ring_hop(1, 1, 1)
    ring_hop(1, 2, 1)
    ring_hop(1, 3, 1)
    ring_hop(1, 0, 2)
    ring_hop(1, 1, 2)
    ring_hop(1, 2, 2)
    ring_hop(1, 3, 2)
    cube_early(0)
    ring_hop(1, 0, 3)
    ring_hop(1, 1, 3)
    ring_hop(1, 2, 3)
    ring_hop(1, 3, 3)
    cube_early(1)
    ring_last(1, 0)
    ring_last(1, 1)
    cube_late(0)
    ring_last(1, 2)
    ring_last(1, 3)
    cube_late(1)

    for i in range(2):
        wait_for(out.at[i, :, 1 - core], out_recv.at[i, 1 - core])

    @pl.when(jnp.logical_not(settled))
    def _():
        for i in range(2):
            wait_for(out.at[i, :, core], out_recv.at[i, core])
            wait_for(obuf.at[i, 1], out_send)
        for c in range(4):
            wait_for(rrecv[c].at[pl.ds(0, 2)], a2a_send.at[0])
        wait_for(crecv.at[pl.ds(0, 2)], a2a_send.at[1])
        wait_for(prow.at[0], a2a_send.at[2])
        wait_for(pcol.at[0], a2a_send.at[2])

    for c in range(4):
        wait_for(rrecv[c].at[pl.ds(0, 30)], a2a_send.at[0])
    wait_for(crecv.at[pl.ds(0, 30)], a2a_send.at[1])
    wait_for(prow.at[pl.ds(1, 15)], a2a_send.at[2])
    wait_for(pcol.at[pl.ds(1, 15)], a2a_send.at[2])
    for i in range(2):
        wait_for(obuf.at[i, 0], out_send)
        wait_for(final.at[i, 1], share_send.at[2 + i])
    for c in range(4):
        wait_for(srecv[c].at[pl.ds(0, 30)], s_send.at[c // 2])
        wait_for(panel.at[c, pl.ds(0, 15)], z_send.at[0, c])
        wait_for(square_panel.at[c, pl.ds(0, 7)], z_send.at[1, c])
    wait_for(pcol, share_send.at[4])
    for j in range(2):
        wait_for(cpanel[j].at[:, pl.ds(0, SLOTS)], share_send.at[j])
        wait_for(cpanel[j].at[pl.ds(0, 15), pl.ds(0, SLOTS)], c_send.at[j])


def shards(density, pattern):
    vmem, smem, dma = pltpu.VMEM, pltpu.SMEM, pltpu.SemaphoreType.DMA
    received = [vmem((NB + 1, PART, HALF), BF16)] * 4
    panel = vmem((GROUP, SLOTS + 1, PART, SIZE), BF16)
    purified = pl.pallas_call(
        kernel,
        out_shape=jax.ShapeDtypeStruct((2, 8, 2, PART, 2 * SIZE), BF16),
        in_specs=[pl.BlockSpec(memory_space=pl.ANY)] * 2,
        out_specs=pl.BlockSpec(memory_space=vmem),
        scratch_shapes=[
            vmem((2, 2, SIZE, SIZE), BF16),
            smem((2, 2), jnp.int32),
            *received, *received,
            vmem((NB + 1, PART, 2 * SIZE), BF16),
            vmem((4, GROUP, PART, SLOTS * HALF), BF16),
            vmem((4, 8, PART, SLOTS * HALF), BF16),
            panel, panel, panel, panel,
            vmem((4, SLOTS * HALF, 4 * SIZE), BF16),
            vmem((2, 8, 2, PART, 2 * SIZE), F32),
            vmem((2, 2, 8, PART, 2 * SIZE), F32),
            vmem((2, 2, SIZE, SIZE), BF16),
            vmem((2, 2, 8, PART, 2 * SIZE), BF16),
            vmem((1, 128), jnp.int32),
            vmem((GROUP, 1, 128), jnp.int32),
            vmem((GROUP, 1, 128), jnp.int32),
            vmem((GROUP, 1, 128), jnp.int32),
            smem((GROUP, 1, 128), jnp.int32),
            smem((GROUP, 1, 128), jnp.int32),
            smem((GROUP, 1, 128), jnp.int32),
            smem((4, NB + 1), jnp.int32),
            smem((4, SLOTS), jnp.int32),
            smem((4, NB + 1), jnp.int32),
            dma((5,)), dma((3,)), dma((4,)), dma, dma((2,)), dma((2,)),
            dma((2,)), dma((4,)), dma((2, 4)), dma((2, 4, 2, 4)), dma((4,)), dma((5,)), dma((5,)),
            dma((2,)), dma((2, 16)), dma, dma((2, 2)),
        ],
        compiler_params=pltpu.CompilerParams(collective_id=0, has_side_effects=True, vmem_limit_bytes=48 * 2**20),
        name="purify",
    )(density.reshape(2, SIZE, 2 * SIZE), pattern)
    return purified.reshape(2 * SIZE, 2 * SIZE)


def solution(mesh):
    return jax.shard_map(
        shards,
        mesh=mesh,
        in_specs=(P("row", "col"), P("row", "col")),
        out_specs=P("row", "col"),
        check_vma=False,
    )
```
